512 devices in a mesh: dp: 32 (over y, z_hi), tensor: 16 (over x, z_lo, core).
Axes of the slice: x: 4, y: 8, z: 8 (z_hi: 4, z_lo: 2; z = z_hi * 2 + z_lo), core: 2. Of those that a mesh axis runs over, the one named last changes fastest.
Arguments:
- hidden: bfloat16 [1024, 5120], P('dp'), may hold values from -6 to 6
- query_base_matrix: bfloat16 [5120, 4096], P(None, 'tensor'), may hold values from -0.078125 to 0.078125
- input_side_factor: bfloat16 [5120, 64], P('dp'), may hold values from -0.078125 to 0.078125
- output_side_factor: bfloat16 [64, 16, 256], P(None, None, 'dp'), may hold values from -0.75 to 0.75
- query_norm_gain: float32 [128], replicated, may hold values from 0.5 to 2
- cached_key_heads: bfloat16 [1024, 16, 64, 128], P('dp', 'tensor'), may hold values from -240 to 240
- cached_value_heads: bfloat16 [1024, 16, 64, 128], P('dp', 'tensor'), may hold values from -6 to 6
- lengths: int32 [1024], P('dp'), may hold values from 1 to 64, as said below
Outputs:
- attended: bfloat16 [1024, 4096], P('dp', 'tensor')
The draws below stay inside these ranges and needn't reach their ends.
Inputs may be any that keep to these rules, and one draw needn't show every extreme that they name: `lengths`: some row holds exactly 64 and some row exactly 1.
All inputs are finite; a program needn't handle non-finite values.
Results may differ from the reference program's by a relative error of at most 0.012.
The reference program's roundings to bfloat16 on the way count: a program that leaves them out, or rounds other values in their place, can miss the bound.
Values may be sent and summed in bfloat16 or wider, within the bound.
A program may use at most 64 MiB of HBM per device.

```python
import math
import jax
import jax.numpy as jnp
from jax import lax

MODEL_WIDTH = 5120
HEAD_SIZE = 128
QUERY_HEADS = 32
ADAPTER_RANK = 64
CTX = 64
ROWS = 32
ROWS_ALL = 1024
QUERY_COLUMNS = 256
N_DP = 32
N_TENSOR = 16


def draw_cached_key_heads(key, part):
    key = jax.random.fold_in(key, 7)
    first = jax.random.fold_in(key, 0)
    dims_all = (ROWS * N_DP, N_TENSOR, CTX, HEAD_SIZE)
    normal_part = jnp.clip(jax.random.normal(first, dims_all, jnp.float32), -6.0, 6.0)
    return normal_part.astype(jnp.bfloat16)


def draw_lengths(key, part):
    key = jax.random.fold_in(key, 11)
    values = jax.random.randint(key, (ROWS * N_DP,), 1, CTX + 1)
    values = values.at[0].set(CTX).at[1].set(1)
    return values.astype(jnp.int32)


def block_levels(key, dims, cuts, least, top_value):
    loudness = 1.0
    for axis_at, blocks in cuts:
        heights = jax.random.uniform(jax.random.fold_in(jax.random.fold_in(key, 6), axis_at), (blocks,), jnp.float32, least / len(cuts), top_value / len(cuts))
        loudness = loudness * jnp.repeat(jnp.exp(heights), dims[axis_at] // blocks).reshape((-1,) + (1,) * (len(dims) - 1 - axis_at))
    return loudness


def gaussian(stream_key, extent, deviation, reach, cuts=(), kind=jnp.bfloat16):
    entries = deviation * jax.random.normal(stream_key, extent, jnp.float32)
    if cuts:
        entries = entries * block_levels(stream_key, extent, cuts, -0.22, 0.18)
    return jnp.clip(entries, -reach, reach).astype(kind)


def setup_inputs(seed: int = 0) -> dict:
    keys = jax.random.split(jax.random.key(seed), 9)
    hidden = gaussian(keys[0], (ROWS_ALL, MODEL_WIDTH), 1.0, 6.0, ((0, 32),))
    query_base_matrix = gaussian(keys[1], (MODEL_WIDTH, QUERY_HEADS * HEAD_SIZE), MODEL_WIDTH ** -0.5, 0.078125, ((1, 16),))
    input_side_factor = gaussian(keys[2], (MODEL_WIDTH, ADAPTER_RANK), MODEL_WIDTH ** -0.5, 0.078125, ((0, 32),))
    output_side_factor = gaussian(keys[3], (ADAPTER_RANK, N_TENSOR, QUERY_COLUMNS), ADAPTER_RANK ** -0.5, 0.75, ((2, 32),))
    query_norm_gain = jnp.clip(jnp.exp(jax.random.uniform(keys[4], (HEAD_SIZE,), jnp.float32, math.log(0.5), math.log(2.0))), 0.5, 2.0)
    cached_key_heads = draw_cached_key_heads(jax.random.fold_in(keys[8], 71), 0)
    cached_value_heads = gaussian(keys[6], (ROWS_ALL, N_TENSOR, CTX, HEAD_SIZE), 1.0, 6.0, ((0, 32), (1, 16)))
    lengths = draw_lengths(jax.random.fold_in(keys[8], 71), 0)
    return {"hidden": hidden, "query_base_matrix": query_base_matrix, "input_side_factor": input_side_factor, "output_side_factor": output_side_factor, "query_norm_gain": query_norm_gain, "cached_key_heads": cached_key_heads, "cached_value_heads": cached_value_heads, "lengths": lengths}


def reference(hidden, query_base_matrix, input_side_factor, output_side_factor, query_norm_gain, cached_key_heads, cached_value_heads, lengths):
    group = QUERY_HEADS // N_TENSOR
    output_factor_slice = output_side_factor.reshape(ADAPTER_RANK, QUERY_HEADS * HEAD_SIZE)
    adapter_update = jnp.dot(input_side_factor, output_factor_slice, preferred_element_type=jnp.float32)
    merged = (query_base_matrix.astype(jnp.float32) + adapter_update).astype(jnp.bfloat16)
    query = jnp.dot(hidden, merged, preferred_element_type=jnp.float32)
    query = query.reshape(hidden.shape[0], N_TENSOR, group, HEAD_SIZE)
    inverse = lax.rsqrt(lax.optimization_barrier(jnp.mean(query * query, axis=-1, keepdims=True)) + 1e-06)
    normed = (query * inverse * query_norm_gain.astype(jnp.float32)).astype(jnp.bfloat16)
    scores = jnp.einsum('rtgd,rtpd->rtgp', normed.astype(jnp.float32), cached_key_heads.astype(jnp.float32)) / math.sqrt(HEAD_SIZE)
    positions = jnp.arange(CTX, dtype=jnp.int32)
    valid = positions[None, None, None, :] < lengths[:, None, None, None]
    scores = jnp.where(valid, scores, -jnp.inf)
    highest = lax.optimization_barrier(jnp.max(scores, axis=-1, keepdims=True))
    expo = jnp.exp(scores - highest)
    weights = (expo / lax.optimization_barrier(jnp.sum(expo, axis=-1, keepdims=True))).astype(jnp.bfloat16)
    result = jnp.einsum('rtgp,rtpd->rtgd', weights.astype(jnp.float32), cached_value_heads.astype(jnp.float32))
    return result.reshape(hidden.shape[0], QUERY_HEADS * HEAD_SIZE).astype(jnp.bfloat16)
```

```python
import functools
import math

import jax
import jax.numpy as jnp
from jax import lax
from jax.experimental import pallas as pl
from jax.experimental.pallas import tpu as pltpu
from jax.sharding import PartitionSpec as P

MESH = pl.DeviceIdType.MESH
N_DP = 32
PACKED = 80
SLOT = PACKED + 32


def flip(bit, other):
    return lax.rem(bit + other, 2)


def bits_of(dp):
    y, zh = dp // 4, lax.rem(dp, 4)
    return y // 4, lax.rem(y // 2, 2), lax.rem(y, 2), zh // 2, lax.rem(zh, 2)


def index_of(y2, y1, y0, z1, z0):
    return y2 * 16 + y1 * 8 + y0 * 4 + z1 * 2 + z0


def source_at(i):
    zh, j = i // 8, lax.rem(i, 8)
    odd = lax.rem(j, 2)
    y = (1 - odd) * (j // 2) + odd * (7 - j // 2)
    return y * 4 + zh


def kernel(
    hidden_hbm, base_hbm, lora_in_hbm, lora_out_hbm, gain_hbm, keys_hbm, values_hbm, lengths_hbm,
    out_ref,
    hidden, base, lora_in, lora_out, gain, keys, values, lengths,
    slots, spread, merged,
    in_sems, send_dp, send_x, send_core, recv,
):
    dp, t = lax.axis_index("dp"), lax.axis_index("tensor")
    x, z_lo, core = t // 4, lax.rem(t // 2, 2), lax.rem(t, 2)
    x1, x0 = x // 2, lax.rem(x, 2)
    y2, y1, y0, z1, z0 = bits_of(dp)
    sibling = (dp, x * 4 + z_lo * 2 + (1 - core))
    x_partners = [(dp, lax.rem(x + d, 4) * 4 + z_lo * 2 + core) for d in (1, 3, 2)]
    dp_partners = [
        (index_of(flip(y2, core), flip(y1, f // 2), flip(y0, f % 2), flip(z1, x0), flip(z0, x1)), t) for f in range(4)
    ]
    own_class = jnp.logical_and(x == 0, core == 0)

    loads = []
    for i, (src, dst) in enumerate(
        (
            (lora_in_hbm, lora_in), (lora_out_hbm, lora_out), (hidden_hbm, hidden), (base_hbm, base),
            (keys_hbm, keys), (values_hbm, values), (gain_hbm, gain), (lengths_hbm, lengths),
        )
    ):
        load = pltpu.make_async_copy(src, dst, in_sems.at[i])
        load.start()
        loads.append(load)

    barrier = pltpu.get_barrier_semaphore()
    for f, partner in enumerate(dp_partners):
        if f == 0:
            @pl.when(jnp.logical_not(own_class))
            def _():
                pl.semaphore_signal(barrier, inc=1, device_id=partner, device_id_type=MESH)
        else:
            pl.semaphore_signal(barrier, inc=1, device_id=partner, device_id_type=MESH)
    for partner in x_partners + [sibling]:
        pl.semaphore_signal(barrier, inc=1, device_id=partner, device_id_type=MESH)

    loads[0].wait()
    loads[1].wait()
    rows = jnp.transpose(lora_in[...].astype(jnp.float32))
    packed = jnp.concatenate([rows[:PACKED], rows[PACKED:]], axis=1)
    ups = []
    for xi in range(4):
        even = lora_out[xi * 4 + z_lo * 2].astype(jnp.float32)
        odd = lora_out[xi * 4 + z_lo * 2 + 1].astype(jnp.float32)
        ups.append(jnp.concatenate([even, odd], axis=1))
    message = jnp.concatenate([ups[0], ups[1], packed, ups[2], ups[3]], axis=0)
    slots[dp] = message.astype(jnp.bfloat16)

    pl.semaphore_wait(barrier, jnp.where(own_class, 7, 8))

    def copy(slot, send_sem, partner):
        return pltpu.make_async_remote_copy(
            src_ref=slots.at[slot], dst_ref=slots.at[slot], send_sem=send_sem, recv_sem=recv.at[slot],
            device_id=partner, device_id_type=MESH,
        )

    for f, partner in enumerate(dp_partners):
        if f == 0:
            @pl.when(jnp.logical_not(own_class))
            def _():
                copy(dp, send_dp.at[f], partner).start()
        else:
            copy(dp, send_dp.at[f], partner).start()

    def roles(i):
        s = source_at(i)
        s2, _, _, sz1, sz0 = bits_of(s)
        same_core = flip(s2, y2) == core
        same_x = jnp.logical_and(flip(sz1, z1) == x0, flip(sz0, z0) == x1)
        same_core = jnp.logical_and(same_core, s != dp)
        return s, same_core, jnp.logical_and(same_core, same_x)

    def arrive(i, _):
        s, same_core, same_plane = roles(i)

        @pl.when(s != dp)
        def _():
            copy(s, send_core.at[s], sibling).wait_recv()

        @pl.when(same_plane)
        def _():
            for k, partner in enumerate(x_partners):
                copy(s, send_x.at[s * 3 + k], partner).start()

        @pl.when(same_core)
        def _():
            copy(s, send_core.at[s], sibling).start()

        return 0

    lax.fori_loop(0, N_DP, arrive, 0)

    group = slots[:, pl.ds((x // 2) * (SLOT - 16), 16), :].astype(jnp.float32)
    both = jnp.where(lax.rem(x, 2) == 0, group[:, :8], group[:, 8:]).reshape(256, 128)
    turned = pltpu.roll(both, 64, 1)
    lane = lax.broadcasted_iota(jnp.int32, (256, 128), 1)
    first = jnp.where(core == 0, both, turned)
    second = jnp.where(core == 0, turned, both)
    spread[:256] = jnp.where(lane < 64, first, 0.0).astype(jnp.bfloat16)
    spread[256:] = jnp.where(lane >= 64, second, 0.0).astype(jnp.bfloat16)

    loads[3].wait()

    def merge(s, _):
        update = lax.dot_general(
            slots[s, 16:16 + PACKED, :], spread[...], (((1,), (1,)), ((), ())), preferred_element_type=jnp.float32
        )
        for half in range(2):
            at = pl.ds(pl.multiple_of(s * 160 + half * PACKED, 16), PACKED)
            merged[at, :] = (base[at, :].astype(jnp.float32) + update[:, half * 256:half * 256 + 256]).astype(jnp.bfloat16)
        return 0

    lax.fori_loop(0, N_DP, merge, 0)

    loads[2].wait()
    query = jnp.dot(hidden[...], merged[...], preferred_element_type=jnp.float32)

    for i in (4, 5, 6, 7):
        loads[i].wait()
    gains = gain[...]
    heads = []
    for h in range(2):
        head = query[:, h * 128:h * 128 + 128]
        inverse = lax.rsqrt(jnp.mean(head * head, axis=-1, keepdims=True) + 1e-06)
        heads.append(head * inverse * gains)
    square = (32, 128)
    on_diagonal = lax.broadcasted_iota(jnp.int32, square, 0) == lax.broadcasted_iota(jnp.int32, square, 1)
    length_row = jnp.concatenate([lengths[...], jnp.zeros((1, 96), jnp.int32)], axis=1).astype(jnp.float32)
    length_column = jnp.sum(jnp.where(on_diagonal, length_row, 0.0), axis=1, keepdims=True).astype(jnp.int32)
    tile = (16, 512)
    row = lax.rem(lax.broadcasted_iota(jnp.int32, tile, 0), 8)
    column = lax.broadcasted_iota(jnp.int32, tile, 1)
    own_row = column // 64 == row
    position = lax.rem(column, 64)
    parts = []
    for j in range(4):
        normed = jnp.concatenate([heads[0][j * 8:j * 8 + 8], heads[1][j * 8:j * 8 + 8]], axis=0).astype(jnp.bfloat16)
        keys_tile = keys[j * 8:j * 8 + 8].reshape(512, 128)
        values_tile = values[j * 8:j * 8 + 8].reshape(512, 128)
        scores = lax.dot_general(
            normed, keys_tile, (((1,), (1,)), ((), ())), preferred_element_type=jnp.float32
        ) / math.sqrt(128)
        length = jnp.concatenate([length_column[j * 8:j * 8 + 8]] * 2, axis=0)
        scores = jnp.where(jnp.logical_and(own_row, position < length), scores, -jnp.inf)
        expo = jnp.exp(scores - jnp.max(scores, axis=-1, keepdims=True))
        weights = (expo / jnp.sum(expo, axis=-1, keepdims=True)).astype(jnp.bfloat16)
        parts.append(jnp.dot(weights, values_tile, preferred_element_type=jnp.float32))
    out_ref[...] = jnp.concatenate(
        [jnp.concatenate([part[h * 8:h * 8 + 8] for part in parts], axis=0) for h in range(2)], axis=1
    ).astype(jnp.bfloat16)

    for f, partner in enumerate(dp_partners):
        if f == 0:
            @pl.when(jnp.logical_not(own_class))
            def _():
                copy(dp, send_dp.at[f], partner).wait_send()
        else:
            copy(dp, send_dp.at[f], partner).wait_send()

    def sent(i, _):
        s, same_core, same_plane = roles(i)

        @pl.when(same_plane)
        def _():
            for k, partner in enumerate(x_partners):
                copy(s, send_x.at[s * 3 + k], partner).wait_send()

        @pl.when(same_core)
        def _():
            copy(s, send_core.at[s], sibling).wait_send()

        return 0

    lax.fori_loop(0, N_DP, sent, 0)


def local(
    hidden, query_base_matrix, input_side_factor, output_side_factor,
    query_norm_gain, cached_key_heads, cached_value_heads, lengths,
):
    bf16 = jnp.bfloat16
    return pl.pallas_call(
        kernel,
        out_shape=jax.ShapeDtypeStruct((32, 256), bf16),
        in_specs=[pl.BlockSpec(memory_space=pl.ANY)] * 8,
        out_specs=pl.BlockSpec(memory_space=pltpu.VMEM),
        scratch_shapes=[
            pltpu.VMEM((32, 5120), bf16),
            pltpu.VMEM((5120, 256), bf16),
            pltpu.VMEM((64, 160), bf16),
            pltpu.VMEM((16, 8, 64), bf16),
            pltpu.VMEM((1, 128), jnp.float32),
            pltpu.VMEM((32, 64, 128), bf16),
            pltpu.VMEM((32, 64, 128), bf16),
            pltpu.VMEM((1, 32), jnp.int32),
            pltpu.VMEM((N_DP, SLOT, 128), bf16),
            pltpu.VMEM((512, 128), bf16),
            pltpu.VMEM((5120, 256), bf16),
            pltpu.SemaphoreType.DMA((8,)),
            pltpu.SemaphoreType.DMA((4,)),
            pltpu.SemaphoreType.DMA((N_DP * 3,)),
            pltpu.SemaphoreType.DMA((N_DP,)),
            pltpu.SemaphoreType.DMA((N_DP,)),
        ],
        compiler_params=pltpu.CompilerParams(
            collective_id=0, has_side_effects=True, vmem_limit_bytes=56 * 2**20
        ),
        cost_estimate=pl.CostEstimate(flops=260_000_000, bytes_accessed=4_200_000, transcendentals=32768),
    )(
        hidden, query_base_matrix, input_side_factor.T, jnp.transpose(output_side_factor, (1, 2, 0)),
        query_norm_gain.reshape(1, 128), cached_key_heads.reshape(32, 64, 128),
        cached_value_heads.reshape(32, 64, 128), lengths.reshape(1, 32),
    )


def solution(mesh):
    in_specs = (
        P("dp", None),
        P(None, "tensor"),
        P("dp", None),
        P(None, None, "dp"),
        P(),
        P("dp", "tensor", None, None),
        P("dp", "tensor", None, None),
        P("dp"),
    )
    return jax.shard_map(local, mesh=mesh, in_specs=in_specs, out_specs=P("dp", "tensor"), check_vma=False)
```

```python
import functools
import math

import jax
import jax.numpy as jnp
from jax import lax
from jax.experimental import pallas as pl
from jax.experimental.pallas import tpu as pltpu
from jax.sharding import PartitionSpec as P

MESH = pl.DeviceIdType.MESH
N_DP = 32
PACKED = 80
SLOT = PACKED + 32


ASSIGN = {"z1": "core"}
BITS = ("y2", "y1", "y0", "z1", "z0")
X_FLIPS = [f for f in (1, 3, 2) if not any(f >> i & 1 and f"x{i}" not in ASSIGN.values() for i in range(2))]
FREE = [b for b in BITS if b not in ASSIGN]


def flip(bit, other):
    return lax.rem(bit + other, 2)


def index_of(bits):
    return bits["y2"] * 16 + bits["y1"] * 8 + bits["y0"] * 4 + bits["z1"] * 2 + bits["z0"]


def sources(dp_bits, plane):
    out = []
    for f in range(2 ** len(FREE)):
        bits = {}
        for b in BITS:
            bits[b] = flip(dp_bits[b], plane[ASSIGN[b]] if b in ASSIGN else f >> FREE.index(b) & 1)
        out.append(index_of(bits))
    return out


def kernel(
    hidden_hbm, base_hbm, lora_in_hbm, lora_out_hbm, gain_hbm, keys_hbm, values_hbm, lengths_hbm,
    out_ref,
    hidden, base, lora_in, lora_out, gain, keys, values, lengths,
    slots, spread, merged,
    in_sems, send_dp, send_x, send_core, recv,
):
    dp, t = lax.axis_index("dp"), lax.axis_index("tensor")
    x, z_lo, core = t // 4, lax.rem(t // 2, 2), lax.rem(t, 2)
    y, z_hi = dp // 4, lax.rem(dp, 4)
    dp_bits = {"y2": y // 4, "y1": lax.rem(y // 2, 2), "y0": lax.rem(y, 2), "z1": z_hi // 2, "z0": lax.rem(z_hi, 2)}
    sibling = (dp, x * 4 + z_lo * 2 + (1 - core))

    def plane(x_flip, core_flip):
        return {
            "x1": flip(x // 2, x_flip // 2), "x0": flip(lax.rem(x, 2), x_flip % 2), "core": flip(core, core_flip),
        }

    def x_partner(x_flip):
        p = plane(x_flip, 0)
        return (dp, (p["x1"] * 2 + p["x0"]) * 4 + z_lo * 2 + core)

    x_partners = [x_partner(f) for f in X_FLIPS]
    direct = sources(dp_bits, plane(0, 0))
    by_x = [s for f in X_FLIPS for s in sources(dp_bits, plane(f, 0))]
    by_core = [s for f in [0] + X_FLIPS for s in sources(dp_bits, plane(f, 1))]

    loads = []
    for i, (src, dst) in enumerate(
        (
            (lora_in_hbm, lora_in), (lora_out_hbm, lora_out), (hidden_hbm, hidden), (base_hbm, base),
            (keys_hbm, keys), (values_hbm, values), (gain_hbm, gain), (lengths_hbm, lengths),
        )
    ):
        load = pltpu.make_async_copy(src, dst, in_sems.at[i])
        load.start()
        loads.append(load)

    barrier = pltpu.get_barrier_semaphore()
    for s in direct:
        @pl.when(s != dp)
        def _():
            pl.semaphore_signal(barrier, inc=1, device_id=(s, t), device_id_type=MESH)
    for partner in x_partners + [sibling]:
        pl.semaphore_signal(barrier, inc=1, device_id=partner, device_id_type=MESH)

    loads[0].wait()
    loads[1].wait()
    rows = jnp.transpose(lora_in[...].astype(jnp.float32))
    packed = jnp.concatenate([rows[:PACKED], rows[PACKED:]], axis=1)
    ups = []
    for xi in range(4):
        even = lora_out[xi * 4 + z_lo * 2].astype(jnp.float32)
        odd = lora_out[xi * 4 + z_lo * 2 + 1].astype(jnp.float32)
        ups.append(jnp.concatenate([even, odd], axis=1))
    message = jnp.concatenate([ups[0], ups[1], packed, ups[2], ups[3]], axis=0)
    slots[dp] = message.astype(jnp.bfloat16)

    n_partners = len(direct) + len(x_partners) + 1
    pl.semaphore_wait(barrier, jnp.where(direct[0] == dp, n_partners - 1, n_partners))

    def copy(slot, send_sem, partner):
        return pltpu.make_async_remote_copy(
            src_ref=slots.at[slot], dst_ref=slots.at[slot], send_sem=send_sem, recv_sem=recv.at[slot],
            device_id=partner, device_id_type=MESH,
        )

    n_direct, n_x = len(direct), len(x_partners)
    for i, s in enumerate(direct):
        @pl.when(s != dp)
        def _():
            copy(dp, send_dp.at[i], (s, t)).start()

    for i, s in enumerate(direct):
        @pl.when(s != dp)
        def _():
            copy(s, send_core.at[i], sibling).wait_recv()
            for k, partner in enumerate(x_partners):
                copy(s, send_x.at[i * n_x + k], partner).start()
            copy(s, send_core.at[i], sibling).start()

    for i, s in enumerate(by_x):
        @pl.when(s != dp)
        def _():
            copy(s, send_core.at[n_direct + i], sibling).wait_recv()
            copy(s, send_core.at[n_direct + i], sibling).start()

    for s in by_core:
        @pl.when(s != dp)
        def _():
            copy(s, send_core.at[0], sibling).wait_recv()

    group = slots[:, pl.ds((x // 2) * (SLOT - 16), 16), :].astype(jnp.float32)
    both = jnp.where(lax.rem(x, 2) == 0, group[:, :8], group[:, 8:]).reshape(256, 128)
    turned = pltpu.roll(both, 64, 1)
    lane = lax.broadcasted_iota(jnp.int32, (128, 256), 0)
    first = jnp.transpose(jnp.where(core == 0, both, turned))
    second = jnp.transpose(jnp.where(core == 0, turned, both))
    spread[:, :256] = jnp.where(lane < 64, first, 0.0).astype(jnp.bfloat16)
    spread[:, 256:] = jnp.where(lane >= 64, second, 0.0).astype(jnp.bfloat16)

    loads[3].wait()

    def merge(s, _):
        update = lax.dot_general(
            slots[s, 16:16 + PACKED, :], spread[...], (((1,), (0,)), ((), ())), preferred_element_type=jnp.float32
        )
        for half in range(2):
            at = pl.ds(pl.multiple_of(s * 160 + half * PACKED, 16), PACKED)
            merged[at, :] = (base[at, :].astype(jnp.float32) + update[:, half * 256:half * 256 + 256]).astype(jnp.bfloat16)
        return 0

    lax.fori_loop(0, N_DP, merge, 0, unroll=True)

    loads[2].wait()
    query = jnp.dot(hidden[...], merged[...], preferred_element_type=jnp.float32)

    for i in (4, 5, 6, 7):
        loads[i].wait()
    gains = gain[...]
    heads = []
    for h in range(2):
        head = query[:, h * 128:h * 128 + 128]
        inverse = lax.rsqrt(jnp.mean(head * head, axis=-1, keepdims=True) + 1e-06)
        heads.append(head * inverse * gains)
    square = (32, 128)
    on_diagonal = lax.broadcasted_iota(jnp.int32, square, 0) == lax.broadcasted_iota(jnp.int32, square, 1)
    length_row = jnp.concatenate([lengths[...], jnp.zeros((1, 96), jnp.int32)], axis=1).astype(jnp.float32)
    length_column = jnp.sum(jnp.where(on_diagonal, length_row, 0.0), axis=1, keepdims=True).astype(jnp.int32)
    tile = (16, 512)
    row = lax.rem(lax.broadcasted_iota(jnp.int32, tile, 0), 8)
    column = lax.broadcasted_iota(jnp.int32, tile, 1)
    own_row = column // 64 == row
    position = lax.rem(column, 64)
    parts = []
    for j in range(4):
        normed = jnp.concatenate([heads[0][j * 8:j * 8 + 8], heads[1][j * 8:j * 8 + 8]], axis=0).astype(jnp.bfloat16)
        keys_tile = keys[j * 8:j * 8 + 8].reshape(512, 128)
        values_tile = values[j * 8:j * 8 + 8].reshape(512, 128)
        scores = lax.dot_general(
            normed, keys_tile, (((1,), (1,)), ((), ())), preferred_element_type=jnp.float32
        ) / math.sqrt(128)
        length = jnp.concatenate([length_column[j * 8:j * 8 + 8]] * 2, axis=0)
        scores = jnp.where(jnp.logical_and(own_row, position < length), scores, -jnp.inf)
        expo = jnp.exp(scores - jnp.max(scores, axis=-1, keepdims=True))
        weights = (expo / jnp.sum(expo, axis=-1, keepdims=True)).astype(jnp.bfloat16)
        parts.append(jnp.dot(weights, values_tile, preferred_element_type=jnp.float32))
    out_ref[...] = jnp.concatenate(
        [jnp.concatenate([part[h * 8:h * 8 + 8] for part in parts], axis=0) for h in range(2)], axis=1
    ).astype(jnp.bfloat16)

    for i, s in enumerate(direct):
        @pl.when(s != dp)
        def _():
            copy(dp, send_dp.at[i], (s, t)).wait_send()
            for k, partner in enumerate(x_partners):
                copy(s, send_x.at[i * n_x + k], partner).wait_send()
            copy(s, send_core.at[i], sibling).wait_send()

    for i, s in enumerate(by_x):
        @pl.when(s != dp)
        def _():
            copy(s, send_core.at[n_direct + i], sibling).wait_send()


def local(
    hidden, query_base_matrix, input_side_factor, output_side_factor,
    query_norm_gain, cached_key_heads, cached_value_heads, lengths,
):
    bf16 = jnp.bfloat16
    return pl.pallas_call(
        kernel,
        out_shape=jax.ShapeDtypeStruct((32, 256), bf16),
        in_specs=[pl.BlockSpec(memory_space=pl.ANY)] * 8,
        out_specs=pl.BlockSpec(memory_space=pltpu.VMEM),
        scratch_shapes=[
            pltpu.VMEM((32, 5120), bf16),
            pltpu.VMEM((5120, 256), bf16),
            pltpu.VMEM((64, 160), bf16),
            pltpu.VMEM((16, 8, 64), bf16),
            pltpu.VMEM((1, 128), jnp.float32),
            pltpu.VMEM((32, 64, 128), bf16),
            pltpu.VMEM((32, 64, 128), bf16),
            pltpu.VMEM((1, 32), jnp.int32),
            pltpu.VMEM((N_DP, SLOT, 128), bf16),
            pltpu.VMEM((128, 512), bf16),
            pltpu.VMEM((5120, 256), bf16),
            pltpu.SemaphoreType.DMA((8,)),
            pltpu.SemaphoreType.DMA((N_DP,)),
            pltpu.SemaphoreType.DMA((N_DP * 3,)),
            pltpu.SemaphoreType.DMA((N_DP,)),
            pltpu.SemaphoreType.DMA((N_DP,)),
        ],
        compiler_params=pltpu.CompilerParams(
            collective_id=0, has_side_effects=True, vmem_limit_bytes=56 * 2**20
        ),
        cost_estimate=pl.CostEstimate(flops=260_000_000, bytes_accessed=4_200_000, transcendentals=32768),
    )(
        hidden, query_base_matrix, input_side_factor.T, jnp.transpose(output_side_factor, (1, 2, 0)),
        query_norm_gain.reshape(1, 128), cached_key_heads.reshape(32, 64, 128),
        cached_value_heads.reshape(32, 64, 128), lengths.reshape(1, 32),
    )


def solution(mesh):
    in_specs = (
        P("dp", None),
        P(None, "tensor"),
        P("dp", None),
        P(None, None, "dp"),
        P(),
        P("dp", "tensor", None, None),
        P("dp", "tensor", None, None),
        P("dp"),
    )
    return jax.shard_map(local, mesh=mesh, in_specs=in_specs, out_specs=P("dp", "tensor"), check_vma=False)
```

```python
import functools
import math

import jax
import jax.numpy as jnp
from jax import lax
from jax.experimental import pallas as pl
from jax.experimental.pallas import tpu as pltpu
from jax.sharding import PartitionSpec as P

MESH = pl.DeviceIdType.MESH
N_DP = 32
PACKED = 80
GROUP = 16
SENT = GROUP + PACKED
SLOT = SENT + GROUP
SERVE_Y = (0, 1, 2, 3, 7, 6, 5, 4)
AWAIT_Y = (0, 1, 7, 2, 6, 3, 5, 4)


def flip(bit, other):
    return lax.rem(bit + other, 2)


def kernel(
    hidden_hbm, base_hbm, lora_in_hbm, lora_out_hbm, gain_hbm, keys_hbm, values_hbm, lengths_hbm,
    out_ref,
    hidden, base, lora_in, lora_out, gain, keys, values, lengths,
    slots, spread, merged,
    in_sems, send_dp, send_core, recv,
):
    dp, t = lax.axis_index("dp"), lax.axis_index("tensor")
    x, z_lo, core = t // 4, lax.rem(t // 2, 2), lax.rem(t, 2)
    z1, z0 = lax.rem(dp // 2, 2), lax.rem(dp, 2)
    sibling = (dp, x * 4 + z_lo * 2 + (1 - core))
    reach = flip(z1, core)

    def partner(y, far):
        swap = core * (1 - flip(z0, far))
        return (y * 4 + reach * 2 + far, x * 4 + flip(z_lo, swap) * 2 + core)

    serve = [partner(y, far) for far in range(2) for y in SERVE_Y]
    direct = [partner(y, far)[0] for far in range(2) for y in AWAIT_Y]
    by_core = [y * 4 + (1 - reach) * 2 + far for far in range(2) for y in AWAIT_Y]

    def load(i):
        src, dst = (
            (lora_in_hbm, lora_in), (lora_out_hbm, lora_out), (hidden_hbm, hidden), (base_hbm, base),
            (keys_hbm, keys), (values_hbm, values), (gain_hbm, gain), (lengths_hbm, lengths),
        )[i]
        return pltpu.make_async_copy(src, dst, in_sems.at[i])

    for i in (0, 1):
        load(i).start()

    barrier = pltpu.get_barrier_semaphore()
    for device in serve:
        @pl.when(device[0] != dp)
        def _():
            pl.semaphore_signal(barrier, inc=1, device_id=device, device_id_type=MESH)
    pl.semaphore_signal(barrier, inc=1, device_id=sibling, device_id_type=MESH)

    load(0).wait()
    load(1).wait()
    rows = jnp.transpose(lora_in[...].astype(jnp.float32))
    packed = jnp.concatenate([rows[:PACKED], rows[PACKED:]], axis=1)
    slots[dp, GROUP:SENT, :] = packed.astype(jnp.bfloat16)
    for group in range(2):
        even = lora_out[x * 4 + group * 2].astype(jnp.float32)
        odd = lora_out[x * 4 + group * 2 + 1].astype(jnp.float32)
        columns = jnp.concatenate([jnp.concatenate([even, odd], axis=1)] * 2, axis=0)
        slots[dp, group * SENT:group * SENT + GROUP, :] = columns.astype(jnp.bfloat16)

    pl.semaphore_wait(barrier, jnp.where(core == 0, 16, 17))

    def copy(slot, send_sem, device):
        group = lax.rem(device[1] // 2, 2)
        rows = pl.ds(pl.multiple_of(group * GROUP, GROUP), SENT)
        return pltpu.make_async_remote_copy(
            src_ref=slots.at[slot, rows], dst_ref=slots.at[slot, rows], send_sem=send_sem, recv_sem=recv.at[slot],
            device_id=device, device_id_type=MESH,
        )

    for i, device in enumerate(serve):
        @pl.when(device[0] != dp)
        def _():
            copy(dp, send_dp.at[i], device).start()

    for i in range(2, 8):
        load(i).start()

    for i, s in enumerate(direct):
        @pl.when(s != dp)
        def _():
            copy(s, send_core.at[i], sibling).wait_recv()
            copy(s, send_core.at[i], sibling).start()

    for s in by_core:
        @pl.when(s != dp)
        def _():
            copy(s, send_core.at[0], sibling).wait_recv()

    group = slots[:, pl.ds(pl.multiple_of(z_lo * SENT, GROUP), GROUP), :].astype(jnp.float32)
    both = group[:, :8].reshape(256, 128)
    turned = pltpu.roll(both, 64, 1)
    lane = lax.broadcasted_iota(jnp.int32, (128, 256), 0)
    first = jnp.transpose(jnp.where(core == 0, both, turned))
    second = jnp.transpose(jnp.where(core == 0, turned, both))
    spread[:, :256] = jnp.where(lane < 64, first, 0.0).astype(jnp.bfloat16)
    spread[:, 256:] = jnp.where(lane >= 64, second, 0.0).astype(jnp.bfloat16)

    load(3).wait()

    def merge(s, _):
        update = lax.dot_general(
            slots[s, GROUP:SENT, :], spread[...], (((1,), (0,)), ((), ())), preferred_element_type=jnp.float32
        )
        for half in range(2):
            at = pl.ds(pl.multiple_of(s * 160 + half * PACKED, 16), PACKED)
            merged[at, :] = (base[at, :].astype(jnp.float32) + update[:, half * 256:half * 256 + 256]).astype(jnp.bfloat16)
        return 0

    lax.fori_loop(0, N_DP, merge, 0, unroll=True)

    load(2).wait()
    query = jnp.dot(hidden[...], merged[...], preferred_element_type=jnp.float32)

    for i in (4, 5, 6, 7):
        load(i).wait()
    gains = gain[...]
    heads = []
    for h in range(2):
        head = query[:, h * 128:h * 128 + 128]
        inverse = lax.rsqrt(jnp.mean(head * head, axis=-1, keepdims=True) + 1e-06)
        heads.append(head * inverse * gains)
    square = (32, 128)
    on_diagonal = lax.broadcasted_iota(jnp.int32, square, 0) == lax.broadcasted_iota(jnp.int32, square, 1)
    length_row = jnp.concatenate([lengths[...], jnp.zeros((1, 96), jnp.int32)], axis=1).astype(jnp.float32)
    length_column = jnp.sum(jnp.where(on_diagonal, length_row, 0.0), axis=1, keepdims=True).astype(jnp.int32)
    tile = (16, 512)
    row = lax.rem(lax.broadcasted_iota(jnp.int32, tile, 0), 8)
    column = lax.broadcasted_iota(jnp.int32, tile, 1)
    own_row = column // 64 == row
    position = lax.rem(column, 64)
    parts = []
    for j in range(4):
        normed = jnp.concatenate([heads[0][j * 8:j * 8 + 8], heads[1][j * 8:j * 8 + 8]], axis=0).astype(jnp.bfloat16)
        keys_tile = keys[j * 8:j * 8 + 8].reshape(512, 128)
        values_tile = values[j * 8:j * 8 + 8].reshape(512, 128)
        scores = lax.dot_general(
            normed, keys_tile, (((1,), (1,)), ((), ())), preferred_element_type=jnp.float32
        ) / math.sqrt(128)
        length = jnp.concatenate([length_column[j * 8:j * 8 + 8]] * 2, axis=0)
        scores = jnp.where(jnp.logical_and(own_row, position < length), scores, -jnp.inf)
        expo = jnp.exp(scores - jnp.max(scores, axis=-1, keepdims=True))
        weights = (expo * (1.0 / jnp.sum(expo, axis=-1, keepdims=True))).astype(jnp.bfloat16)
        parts.append(jnp.dot(weights, values_tile, preferred_element_type=jnp.float32))
    out_ref[...] = jnp.concatenate(
        [jnp.concatenate([part[h * 8:h * 8 + 8] for part in parts], axis=0) for h in range(2)], axis=1
    ).astype(jnp.bfloat16)

    for i, device in enumerate(serve):
        @pl.when(device[0] != dp)
        def _():
            copy(dp, send_dp.at[i], device).wait_send()

    for i, s in enumerate(direct):
        @pl.when(s != dp)
        def _():
            copy(s, send_core.at[i], sibling).wait_send()


def local(
    hidden, query_base_matrix, input_side_factor, output_side_factor,
    query_norm_gain, cached_key_heads, cached_value_heads, lengths,
):
    bf16 = jnp.bfloat16
    return pl.pallas_call(
        kernel,
        out_shape=jax.ShapeDtypeStruct((32, 256), bf16),
        in_specs=[pl.BlockSpec(memory_space=pl.ANY)] * 8,
        out_specs=pl.BlockSpec(memory_space=pltpu.VMEM),
        scratch_shapes=[
            pltpu.VMEM((32, 5120), bf16),
            pltpu.VMEM((5120, 256), bf16),
            pltpu.VMEM((64, 160), bf16),
            pltpu.VMEM((16, 8, 64), bf16),
            pltpu.VMEM((1, 128), jnp.float32),
            pltpu.VMEM((32, 64, 128), bf16),
            pltpu.VMEM((32, 64, 128), bf16),
            pltpu.VMEM((1, 32), jnp.int32),
            pltpu.VMEM((N_DP, SLOT, 128), bf16),
            pltpu.VMEM((128, 512), bf16),
            pltpu.VMEM((5120, 256), bf16),
            pltpu.SemaphoreType.DMA((8,)),
            pltpu.SemaphoreType.DMA((16,)),
            pltpu.SemaphoreType.DMA((16,)),
            pltpu.SemaphoreType.DMA((N_DP,)),
        ],
        compiler_params=pltpu.CompilerParams(
            collective_id=0, has_side_effects=True, vmem_limit_bytes=56 * 2**20
        ),
        cost_estimate=pl.CostEstimate(flops=260_000_000, bytes_accessed=4_200_000, transcendentals=32768),
    )(
        hidden, query_base_matrix, input_side_factor.T, jnp.transpose(output_side_factor, (1, 2, 0)),
        query_norm_gain.reshape(1, 128), cached_key_heads.reshape(32, 64, 128),
        cached_value_heads.reshape(32, 64, 128), lengths.reshape(1, 32),
    )


def solution(mesh):
    in_specs = (
        P("dp", None),
        P(None, "tensor"),
        P("dp", None),
        P(None, None, "dp"),
        P(),
        P("dp", "tensor", None, None),
        P("dp", "tensor", None, None),
        P("dp"),
    )
    return jax.shard_map(local, mesh=mesh, in_specs=in_specs, out_specs=P("dp", "tensor"), check_vma=False)
```

```python
import functools
import math

import jax
import jax.numpy as jnp
from jax import lax
from jax.experimental import pallas as pl
from jax.experimental.pallas import tpu as pltpu
from jax.sharding import PartitionSpec as P

MESH = pl.DeviceIdType.MESH
N_DP = 32
PACKED = 80
GROUP = 16
X_FLIPS = (2, 1, 3)
UPPER_Y = (0, 1, 3, 2)


def flip(bit, other):
    return lax.rem(bit + other, 2)


def kernel(
    hidden_hbm, base_hbm, lora_in_hbm, lora_out_hbm, gain_hbm, keys_hbm, values_hbm, lengths_hbm,
    out_ref,
    hidden, base, lora_in, lora_out, gain, keys, values, lengths,
    slots, ups, own_ups, spread, merged,
    in_sems, send_dp, send_x, send_core, recv,
):
    dp, t = lax.axis_index("dp"), lax.axis_index("tensor")
    x, z_lo, core = t // 4, lax.rem(t // 2, 2), lax.rem(t, 2)
    z1, z0 = lax.rem(dp // 2, 2), lax.rem(dp, 2)
    sibling = (dp, x * 4 + z_lo * 2 + (1 - core))
    y0, x1, x0 = lax.rem(dp // 4, 2), x // 2, lax.rem(x, 2)
    early, late = z1 == 0, z1 == 1
    sender = jnp.logical_and(late, core == 1)
    taker = jnp.logical_not(sender)
    both_halves = jnp.logical_and(late, core == 0)
    reach = flip(z1, core)

    def shards(half, x_flip):
        odd, z = flip(y0, flip(x1, x_flip // 2)), flip(z0, flip(x0, x_flip % 2))
        return [(upper * 2 + odd) * 4 + half * 2 + z for upper in UPPER_Y]

    def devices(half, to_core):
        swap = flip(z1, half) * (1 - x0)
        return [(s, x * 4 + flip(z_lo, swap) * 2 + to_core) for s in shards(half, 0)]

    x_partners = [(dp, (flip(x1, f // 2) * 2 + flip(x0, f % 2)) * 4 + z_lo * 2 + core) for f in X_FLIPS]
    serve = devices(reach, core * z1)

    def load(i):
        src, dst = (
            (lora_in_hbm, lora_in), (lora_out_hbm, lora_out), (hidden_hbm, hidden), (base_hbm, base),
            (keys_hbm, keys), (values_hbm, values), (gain_hbm, gain), (lengths_hbm, lengths),
        )[i]
        return pltpu.make_async_copy(src, dst, in_sems.at[i])

    for i in (0, 1):
        load(i).start()

    barrier = pltpu.get_barrier_semaphore()

    def signal(device):
        pl.semaphore_signal(barrier, inc=1, device_id=device, device_id_type=MESH)

    @pl.when(taker)
    def _():
        for device in devices(reach, core):
            @pl.when(device[0] != dp)
            def _():
                signal(device)
        for device in x_partners:
            signal(device)

    @pl.when(both_halves)
    def _():
        for device in devices(0, 1):
            signal(device)

    @pl.when(jnp.logical_not(both_halves))
    def _():
        signal(sibling)

    @pl.when(early)
    def _():
        for i in range(2, 8):
            load(i).start()

    load(0).wait()
    load(1).wait()
    rows = jnp.transpose(lora_in[...].astype(jnp.float32))
    packed = jnp.concatenate([rows[:PACKED], rows[PACKED:]], axis=1)
    slots[dp] = packed.astype(jnp.bfloat16)
    for group in range(2):
        rows = []
        for xi in range(4):
            even = lora_out[xi * 4 + group * 2].astype(jnp.float32)
            odd = lora_out[xi * 4 + group * 2 + 1].astype(jnp.float32)
            rows.append(jnp.concatenate([even, odd], axis=1))
        own_ups[group] = jnp.concatenate(rows, axis=0).astype(jnp.bfloat16)
    ups[dp] = own_ups[z_lo]

    own_class = jnp.logical_and(x == 0, core == 0)
    pl.semaphore_wait(barrier, jnp.where(sender, 4, jnp.where(own_class, 7, 8)))

    def remote(src, dst, send_sem, recv_sem, device):
        return pltpu.make_async_remote_copy(
            src_ref=src, dst_ref=dst, send_sem=send_sem, recv_sem=recv_sem, device_id=device, device_id_type=MESH
        )

    def down(s, send_sem, device):
        return remote(slots.at[s], slots.at[s], send_sem.at[0], recv.at[0, s], device)

    def own_up(send_sem, device):
        z_lo_there = lax.rem(device[1] // 2, 2)
        return remote(own_ups.at[z_lo_there], ups.at[dp], send_sem.at[1], recv.at[1, dp], device)

    def up(s, send_sem, device):
        rows = pl.ds(pl.multiple_of(device[1] // 8 * GROUP, GROUP), GROUP)
        return remote(ups.at[s, rows], ups.at[s, rows], send_sem.at[1], recv.at[1, s], device)

    def serve_each(act):
        for i, device in enumerate(serve):
            @pl.when(device[0] != dp)
            def _():
                act(send_dp.at[i], device)

    serve_each(lambda sem, device: own_up(sem, device).start())
    serve_each(lambda sem, device: down(dp, sem, device).start())

    @pl.when(late)
    def _():
        for i in range(2, 8):
            load(i).start()

    def each(half, x_flips, act):
        for j, f in enumerate(x_flips):
            for i, s in enumerate(shards(half, f)):
                @pl.when(s != dp)
                def _():
                    act(s, j * 4 + i)

    def halves(act):
        @pl.when(taker)
        def _():
            act(reach, 0)

        @pl.when(both_halves)
        def _():
            act(0, 1)

    def take(kind, arrival):
        def take_half(half, n):
            def act(s, i):
                arrival(s).wait_recv()
                for k, device in enumerate(x_partners):
                    kind(s, send_x.at[n * 12 + i * 3 + k], device).start()
                kind(s, send_core.at[n * 16 + i], sibling).start()

            each(half, (0,), act)

        halves(take_half)

    def pass_on(kind):
        def pass_half(half, n):
            def act(s, i):
                kind(s, send_core.at[0], sibling).wait_recv()
                kind(s, send_core.at[n * 16 + 4 + i], sibling).start()

            each(half, X_FLIPS, act)

        halves(pass_half)

    def from_sibling(kind):
        def wait_half(half):
            for i in range(16):
                s = (i // 2) * 4 + half * 2 + i % 2

                @pl.when(s != dp)
                def _():
                    kind(s, send_core.at[0], sibling).wait_recv()

        @pl.when(jnp.logical_not(both_halves))
        def _():
            wait_half(1 - reach)

        @pl.when(sender)
        def _():
            wait_half(reach)

    take(up, lambda s: remote(own_ups.at[z_lo], ups.at[s], send_dp.at[0, 1], recv.at[1, s], sibling))
    take(down, lambda s: down(s, send_core.at[0], sibling))
    pass_on(up)
    pass_on(down)
    from_sibling(up)
    from_sibling(down)

    pair = ups[:, pl.ds(pl.multiple_of(x1 * GROUP, GROUP), GROUP), :].astype(jnp.float32)
    both = jnp.where(x0 == 0, pair[:, :8], pair[:, 8:]).reshape(256, 128)
    turned = pltpu.roll(both, 64, 1)
    lane = lax.broadcasted_iota(jnp.int32, (128, 256), 0)
    first = jnp.transpose(jnp.where(core == 0, both, turned))
    second = jnp.transpose(jnp.where(core == 0, turned, both))
    spread[:, :256] = jnp.where(lane < 64, first, 0.0).astype(jnp.bfloat16)
    spread[:, 256:] = jnp.where(lane >= 64, second, 0.0).astype(jnp.bfloat16)

    load(3).wait()

    def merge(s, _):
        update = lax.dot_general(
            slots[s], spread[...], (((1,), (0,)), ((), ())), preferred_element_type=jnp.float32
        )
        for half in range(2):
            at = pl.ds(pl.multiple_of(s * 160 + half * PACKED, 16), PACKED)
            merged[at, :] = (base[at, :].astype(jnp.float32) + update[:, half * 256:half * 256 + 256]).astype(jnp.bfloat16)
        return 0

    lax.fori_loop(0, N_DP, merge, 0, unroll=True)

    load(2).wait()
    query = jnp.dot(hidden[...], merged[...], preferred_element_type=jnp.float32)

    for i in (4, 5, 6, 7):
        load(i).wait()
    gains = gain[...]
    heads = []
    for h in range(2):
        head = query[:, h * 128:h * 128 + 128]
        inverse = lax.rsqrt(jnp.mean(head * head, axis=-1, keepdims=True) + 1e-06)
        heads.append(head * inverse * gains)
    square = (32, 128)
    on_diagonal = lax.broadcasted_iota(jnp.int32, square, 0) == lax.broadcasted_iota(jnp.int32, square, 1)
    length_row = jnp.concatenate([lengths[...], jnp.zeros((1, 96), jnp.int32)], axis=1).astype(jnp.float32)
    length_column = jnp.sum(jnp.where(on_diagonal, length_row, 0.0), axis=1, keepdims=True).astype(jnp.int32)
    tile = (16, 512)
    row = lax.rem(lax.broadcasted_iota(jnp.int32, tile, 0), 8)
    column = lax.broadcasted_iota(jnp.int32, tile, 1)
    own_row = column // 64 == row
    position = lax.rem(column, 64)
    parts = []
    for j in range(4):
        normed = jnp.concatenate([heads[0][j * 8:j * 8 + 8], heads[1][j * 8:j * 8 + 8]], axis=0).astype(jnp.bfloat16)
        keys_tile = keys[j * 8:j * 8 + 8].reshape(512, 128)
        values_tile = values[j * 8:j * 8 + 8].reshape(512, 128)
        scores = lax.dot_general(
            normed, keys_tile, (((1,), (1,)), ((), ())), preferred_element_type=jnp.float32
        ) / math.sqrt(128)
        length = jnp.concatenate([length_column[j * 8:j * 8 + 8]] * 2, axis=0)
        scores = jnp.where(jnp.logical_and(own_row, position < length), scores, -jnp.inf)
        expo = jnp.exp(scores - jnp.max(scores, axis=-1, keepdims=True))
        weights = (expo * (1.0 / jnp.sum(expo, axis=-1, keepdims=True))).astype(jnp.bfloat16)
        parts.append(jnp.dot(weights, values_tile, preferred_element_type=jnp.float32))
    out_ref[...] = jnp.concatenate(
        [jnp.concatenate([part[h * 8:h * 8 + 8] for part in parts], axis=0) for h in range(2)], axis=1
    ).astype(jnp.bfloat16)

    serve_each(lambda sem, device: own_up(sem, device).wait_send())
    serve_each(lambda sem, device: down(dp, sem, device).wait_send())

    def sent(half, n):
        def direct(s, i):
            for k, device in enumerate(x_partners):
                for kind in (up, down):
                    kind(s, send_x.at[n * 12 + i * 3 + k], device).wait_send()

        def every(s, i):
            for kind in (up, down):
                kind(s, send_core.at[n * 16 + i], sibling).wait_send()

        each(half, (0,), direct)
        each(half, (0,) + X_FLIPS, every)

    halves(sent)


def local(
    hidden, query_base_matrix, input_side_factor, output_side_factor,
    query_norm_gain, cached_key_heads, cached_value_heads, lengths,
):
    bf16 = jnp.bfloat16
    return pl.pallas_call(
        kernel,
        out_shape=jax.ShapeDtypeStruct((32, 256), bf16),
        in_specs=[pl.BlockSpec(memory_space=pl.ANY)] * 8,
        out_specs=pl.BlockSpec(memory_space=pltpu.VMEM),
        scratch_shapes=[
            pltpu.VMEM((32, 5120), bf16),
            pltpu.VMEM((5120, 256), bf16),
            pltpu.VMEM((64, 160), bf16),
            pltpu.VMEM((16, 8, 64), bf16),
            pltpu.VMEM((1, 128), jnp.float32),
            pltpu.VMEM((32, 64, 128), bf16),
            pltpu.VMEM((32, 64, 128), bf16),
            pltpu.VMEM((1, 32), jnp.int32),
            pltpu.VMEM((N_DP, PACKED, 128), bf16),
            pltpu.VMEM((N_DP, 2 * GROUP, 128), bf16),
            pltpu.VMEM((2, 2 * GROUP, 128), bf16),
            pltpu.VMEM((128, 512), bf16),
            pltpu.VMEM((5120, 256), bf16),
            pltpu.SemaphoreType.DMA((8,)),
            pltpu.SemaphoreType.DMA((4, 2)),
            pltpu.SemaphoreType.DMA((24, 2)),
            pltpu.SemaphoreType.DMA((32, 2)),
            pltpu.SemaphoreType.DMA((2, N_DP)),
        ],
        compiler_params=pltpu.CompilerParams(
            collective_id=0, has_side_effects=True, vmem_limit_bytes=56 * 2**20
        ),
        cost_estimate=pl.CostEstimate(flops=260_000_000, bytes_accessed=4_200_000, transcendentals=32768),
    )(
        hidden, query_base_matrix, input_side_factor.T, jnp.transpose(output_side_factor, (1, 2, 0)),
        query_norm_gain.reshape(1, 128), cached_key_heads.reshape(32, 64, 128),
        cached_value_heads.reshape(32, 64, 128), lengths.reshape(1, 32),
    )


def solution(mesh):
    in_specs = (
        P("dp", None),
        P(None, "tensor"),
        P("dp", None),
        P(None, None, "dp"),
        P(),
        P("dp", "tensor", None, None),
        P("dp", "tensor", None, None),
        P("dp"),
    )
    return jax.shard_map(local, mesh=mesh, in_specs=in_specs, out_specs=P("dp", "tensor"), check_vma=False)
```

```python
import functools
import math

import jax
import jax.numpy as jnp
from jax import lax
from jax.experimental import pallas as pl
from jax.experimental.pallas import tpu as pltpu
from jax.sharding import PartitionSpec as P

MESH = pl.DeviceIdType.MESH
N_DP = 32
PACKED = 80
GROUP = 16
SERVE_Y = (0, 1, 2, 3, 7, 6, 5, 4)
AWAIT_Y = (0, 1, 7, 2, 6, 3, 5, 4)


def flip(bit, other):
    return lax.rem(bit + other, 2)


def group(g):
    return [[y * 4 + half * 2 + g // 2 for half in range(2)] for y in AWAIT_Y[g % 2 * 4:g % 2 * 4 + 4]]


def kernel(
    hidden_hbm, base_hbm, lora_in_hbm, lora_out_hbm, gain_hbm, keys_hbm, values_hbm, lengths_hbm,
    out_ref,
    hidden, base, lora_in, lora_out, gain, keys, values, lengths,
    slots, ups, spread, merged, ordered, turned_keys, bias,
    in_sems, send_dp, send_pair, send_core, recv,
):
    dp, t = lax.axis_index("dp"), lax.axis_index("tensor")
    x, z_lo, core = t // 4, lax.rem(t // 2, 2), lax.rem(t, 2)
    z1, z0 = lax.rem(dp // 2, 2), lax.rem(dp, 2)
    sibling = (dp, x * 4 + z_lo * 2 + (1 - core))
    early, late = z1 == 0, z1 == 1
    early_0, early_1 = jnp.logical_and(early, core == 0), jnp.logical_and(early, core == 1)
    late_0, late_1 = jnp.logical_and(late, core == 0), jnp.logical_and(late, core == 1)
    pair = (dp, x * 4 + (1 - z_lo) * 2 + core)

    def at(y, z_hi, lo, to_core):
        return (y * 4 + z_hi, x * 4 + lo * 2 + to_core)

    def within(half):
        return [at(y, half * 2 + z, z_lo, 0) for z in range(2) for y in SERVE_Y]

    def across(half, to_core):
        return [at(y, half * 2 + z, flip(z_lo, flip(z0, z + 1)), to_core) for z in range(2) for y in SERVE_Y]

    def late_sender(y):
        z = 1 - z_lo
        return at(y, 2 + z, z + z0 - z * z0, 1)

    late_serves = [(at(y, z, 1 - z0, 1), z0 + z - z0 * z == z_lo) for z in range(2) for y in SERVE_Y]
    n_late_serves = jnp.where(z0 == 0, 8, jnp.where(z_lo == 1, 16, 0))

    def load(i):
        src, dst = (
            (lora_in_hbm, lora_in), (lora_out_hbm, lora_out), (hidden_hbm, hidden), (base_hbm, base),
            (keys_hbm, keys), (values_hbm, values), (gain_hbm, gain), (lengths_hbm, lengths),
        )[i]
        return pltpu.make_async_copy(src, dst, in_sems.at[i])

    for i in (0, 1):
        load(i).start()

    barrier = pltpu.get_barrier_semaphore()

    def signal(device):
        pl.semaphore_signal(barrier, inc=1, device_id=device, device_id_type=MESH)

    @pl.when(core == 0)
    def _():
        for device in within(z1):
            @pl.when(device[0] != dp)
            def _():
                signal(device)

    @pl.when(late_0)
    def _():
        for device in across(0, 1):
            signal(device)

    @pl.when(early_1)
    def _():
        for y in AWAIT_Y:
            signal(late_sender(y))
        signal(pair)

    @pl.when(jnp.logical_not(late_0))
    def _():
        signal(sibling)

    @pl.when(early)
    def _():
        for i in range(2, 8):
            load(i).start()

    load(0).wait()
    load(1).wait()
    rows = jnp.transpose(lora_in[...].astype(jnp.float32))
    packed = jnp.concatenate([rows[:PACKED], rows[PACKED:]], axis=1)
    slots[dp] = packed.astype(jnp.bfloat16)
    columns = []
    for lo in range(2):
        even = lora_out[x * 4 + lo * 2].astype(jnp.float32)
        odd = lora_out[x * 4 + lo * 2 + 1].astype(jnp.float32)
        columns.append(jnp.concatenate([even, odd], axis=1))
    ups[dp] = jnp.concatenate(columns, axis=0).astype(jnp.bfloat16)

    def prepare():
        for i in range(4, 8):
            load(i).wait()
        square = (32, 128)
        on_diagonal = lax.broadcasted_iota(jnp.int32, square, 0) == lax.broadcasted_iota(jnp.int32, square, 1)
        length_row = jnp.concatenate([lengths[...], jnp.zeros((1, 96), jnp.int32)], axis=1).astype(jnp.float32)
        length_column = jnp.sum(jnp.where(on_diagonal, length_row, 0.0), axis=1, keepdims=True).astype(jnp.int32)
        tile = (16, 512)
        row = lax.rem(lax.broadcasted_iota(jnp.int32, tile, 0), 8)
        column = lax.broadcasted_iota(jnp.int32, tile, 1)
        own_row = column // 64 == row
        position = lax.rem(column, 64)
        for j in range(4):
            length = jnp.concatenate([length_column[j * 8:j * 8 + 8]] * 2, axis=0)
            bias[j] = jnp.where(jnp.logical_and(own_row, position < length), 0.0, -jnp.inf)
            turned_keys[j] = jnp.transpose(keys[j * 8:j * 8 + 8].reshape(512, 128))
        load(2).wait()
        for g in range(4):
            pieces = [hidden[:, s * 160:s * 160 + 160].astype(jnp.float32) for pair_of in group(g) for s in pair_of]
            ordered[g] = jnp.concatenate(pieces, axis=1).astype(jnp.bfloat16)
        load(3).wait()

    @pl.when(early)
    def _():
        prepare()

    @pl.when(jnp.logical_or(jnp.logical_not(late_1), n_late_serves > 0))
    def _():
        pl.semaphore_wait(barrier, jnp.where(core == 0, 16, jnp.where(early, 18, n_late_serves)))

    def remote(src, dst, send_sem, recv_sem, device):
        return pltpu.make_async_remote_copy(
            src_ref=src, dst_ref=dst, send_sem=send_sem, recv_sem=recv_sem, device_id=device, device_id_type=MESH
        )

    def down(s, send_sem, device):
        return remote(slots.at[s], slots.at[s], send_sem.at[0], recv.at[0, s], device)

    def up(s, send_sem, device):
        return remote(ups.at[s], ups.at[s], send_sem.at[1], recv.at[1, s], device)

    def serve(act):
        @pl.when(late_1)
        def _():
            for i, (device, ours) in enumerate(late_serves):
                @pl.when(ours)
                def _():
                    act(send_dp.at[i], device)

        @pl.when(early_1)
        def _():
            for i, device in enumerate(across(1, 0)):
                act(send_dp.at[i], device)

        @pl.when(core == 0)
        def _():
            for i, device in enumerate(within(z1)):
                @pl.when(device[0] != dp)
                def _():
                    act(send_dp.at[i], device)

    serve(lambda sem, device: up(dp, sem, device).start())
    serve(lambda sem, device: down(dp, sem, device).start())

    @pl.when(late)
    def _():
        for i in range(2, 8):
            load(i).start()

    def half_shards(half):
        return [y * 4 + half * 2 + z for z in range(2) for y in AWAIT_Y]

    def arrive(kind, s):
        kind(s, send_core.at[0], sibling).wait_recv()

    def forward_own(kind, act):
        @pl.when(core == 0)
        def _():
            for i, s in enumerate(half_shards(z1)):
                @pl.when(s != dp)
                def _():
                    act(kind, s, i)

    def forward_other(kind, act, s, i):
        @pl.when(late_0)
        def _():
            act(kind, s, 16 + i)

        @pl.when(early_1)
        def _():
            act(kind, s, i)

            @pl.when(i // 8 != z_lo)
            def _():
                act(kind, s, i, True)

    def pass_on(kind, s, i, to_pair=False):
        if to_pair:
            kind(s, send_pair.at[i % 8], pair).start()
        else:
            arrive(kind, s)
            kind(s, send_core.at[i], sibling).start()

    others = half_shards(1 - z1)
    forward_own(up, pass_on)
    forward_own(down, pass_on)

    @pl.when(late)
    def _():
        prepare()

    for i, s in enumerate(others):
        forward_other(up, pass_on, s, i)

    def from_sibling(kind, s):
        @pl.when(jnp.logical_and(core == 1, s != dp))
        def _():
            arrive(kind, s)

    def others_from_sibling(kind, s):
        @pl.when(jnp.logical_or(early_0, late_1))
        def _():
            arrive(kind, s)

    for s in half_shards(z1):
        from_sibling(up, s)
    for s in others:
        others_from_sibling(up, s)

    lows = ups[...].astype(jnp.float32)
    both = jnp.where(z_lo == 0, lows[:, :8], lows[:, 8:]).reshape(256, 128)
    turned = pltpu.roll(both, 64, 1)
    lane = lax.broadcasted_iota(jnp.int32, (128, 256), 0)
    first = jnp.transpose(jnp.where(core == 0, both, turned))
    second = jnp.transpose(jnp.where(core == 0, turned, both))
    spread[:, :256] = jnp.where(lane < 64, first, 0.0).astype(jnp.bfloat16)
    spread[:, 256:] = jnp.where(lane >= 64, second, 0.0).astype(jnp.bfloat16)

    query = jnp.zeros((32, 256), jnp.float32)
    for g in range(4):
        for k in range(4):
            i = g * 4 + k
            from_sibling(down, half_shards(z1)[i])
            forward_other(down, pass_on, others[i], i)
            others_from_sibling(down, others[i])
        for k, pair_of in enumerate(group(g)):
            for half, s in enumerate(pair_of):
                update = jnp.dot(slots[s], spread[...], preferred_element_type=jnp.float32)
                for part in range(2):
                    base_part = base[s * 160 + part * PACKED:s * 160 + part * PACKED + PACKED].astype(jnp.float32)
                    row = (k * 2 + half) * 160 + part * PACKED
                    merged[g, row:row + PACKED] = (base_part + update[:, part * 256:part * 256 + 256]).astype(jnp.bfloat16)
        query += jnp.dot(ordered[g], merged[g], preferred_element_type=jnp.float32)

    gains = gain[...]
    heads = []
    for h in range(2):
        head = query[:, h * 128:h * 128 + 128]
        inverse = lax.rsqrt(jnp.mean(head * head, axis=-1, keepdims=True) + 1e-06)
        heads.append(head * inverse * gains)
    parts = []
    for j in range(4):
        normed = jnp.concatenate([heads[0][j * 8:j * 8 + 8], heads[1][j * 8:j * 8 + 8]], axis=0).astype(jnp.bfloat16)
        values_tile = values[j * 8:j * 8 + 8].reshape(512, 128)
        scores = jnp.dot(normed, turned_keys[j], preferred_element_type=jnp.float32) / math.sqrt(128) + bias[j]
        expo = jnp.exp(scores - jnp.max(scores, axis=-1, keepdims=True))
        weights = (expo * (1.0 / jnp.sum(expo, axis=-1, keepdims=True))).astype(jnp.bfloat16)
        parts.append(jnp.dot(weights, values_tile, preferred_element_type=jnp.float32))
    out_ref[...] = jnp.concatenate(
        [jnp.concatenate([part[h * 8:h * 8 + 8] for part in parts], axis=0) for h in range(2)], axis=1
    ).astype(jnp.bfloat16)

    serve(lambda sem, device: up(dp, sem, device).wait_send())
    serve(lambda sem, device: down(dp, sem, device).wait_send())

    def sent(kind, s, i, to_pair=False):
        if to_pair:
            kind(s, send_pair.at[i % 8], pair).wait_send()
        else:
            kind(s, send_core.at[i], sibling).wait_send()

    for kind in (up, down):
        forward_own(kind, sent)
        for i, s in enumerate(others):
            forward_other(kind, sent, s, i)


def local(
    hidden, query_base_matrix, input_side_factor, output_side_factor,
    query_norm_gain, cached_key_heads, cached_value_heads, lengths,
):
    bf16 = jnp.bfloat16
    return pl.pallas_call(
        kernel,
        out_shape=jax.ShapeDtypeStruct((32, 256), bf16),
        in_specs=[pl.BlockSpec(memory_space=pl.ANY)] * 8,
        out_specs=pl.BlockSpec(memory_space=pltpu.VMEM),
        scratch_shapes=[
            pltpu.VMEM((32, 5120), bf16),
            pltpu.VMEM((5120, 256), bf16),
            pltpu.VMEM((64, 160), bf16),
            pltpu.VMEM((16, 8, 64), bf16),
            pltpu.VMEM((1, 128), jnp.float32),
            pltpu.VMEM((32, 64, 128), bf16),
            pltpu.VMEM((32, 64, 128), bf16),
            pltpu.VMEM((1, 32), jnp.int32),
            pltpu.VMEM((N_DP, PACKED, 128), bf16),
            pltpu.VMEM((N_DP, GROUP, 128), bf16),
            pltpu.VMEM((128, 512), bf16),
            pltpu.VMEM((4, 1280, 256), bf16),
            pltpu.VMEM((4, 32, 1280), bf16),
            pltpu.VMEM((4, 128, 512), bf16),
            pltpu.VMEM((4, 16, 512), jnp.float32),
            pltpu.SemaphoreType.DMA((8,)),
            pltpu.SemaphoreType.DMA((16, 2)),
            pltpu.SemaphoreType.DMA((8, 2)),
            pltpu.SemaphoreType.DMA((32, 2)),
            pltpu.SemaphoreType.DMA((2, N_DP)),
        ],
        compiler_params=pltpu.CompilerParams(
            collective_id=0, has_side_effects=True, vmem_limit_bytes=56 * 2**20
        ),
        cost_estimate=pl.CostEstimate(flops=260_000_000, bytes_accessed=4_200_000, transcendentals=32768),
    )(
        hidden, query_base_matrix, input_side_factor.T, jnp.transpose(output_side_factor, (1, 2, 0)),
        query_norm_gain.reshape(1, 128), cached_key_heads.reshape(32, 64, 128),
        cached_value_heads.reshape(32, 64, 128), lengths.reshape(1, 32),
    )


def solution(mesh):
    in_specs = (
        P("dp", None),
        P(None, "tensor"),
        P("dp", None),
        P(None, None, "dp"),
        P(),
        P("dp", "tensor", None, None),
        P("dp", "tensor", None, None),
        P("dp"),
    )
    return jax.shard_map(local, mesh=mesh, in_specs=in_specs, out_specs=P("dp", "tensor"), check_vma=False)
```

```python
import functools
import math

import jax
import jax.numpy as jnp
from jax import lax
from jax.experimental import pallas as pl
from jax.experimental.pallas import tpu as pltpu
from jax.sharding import PartitionSpec as P

MESH = pl.DeviceIdType.MESH
N_DP = 32
PACKED = 80
GROUP = 16
SERVE_Y = (0, 1, 2, 3, 7, 6, 5, 4)
AWAIT_Y = (0, 1, 7, 2, 6, 3, 5, 4)


def flip(bit, other):
    return lax.rem(bit + other, 2)


def chunk(half, z):
    return [y * 4 + half * 2 + z for y in AWAIT_Y]


def kernel(
    hidden_hbm, base_hbm, lora_in_hbm, lora_out_hbm, gain_hbm, keys_hbm, values_hbm, lengths_hbm,
    out_ref,
    hidden, base, lora_in, lora_out, gain, keys, values, lengths,
    slots, ups, own_ups, spread, merged, ordered, turned_keys, bias,
    in_sems, send_dp, send_pair, send_core, recv,
):
    dp, t = lax.axis_index("dp"), lax.axis_index("tensor")
    x, z_lo, core = t // 4, lax.rem(t // 2, 2), lax.rem(t, 2)
    z1, z0 = lax.rem(dp // 2, 2), lax.rem(dp, 2)
    sibling = (dp, x * 4 + z_lo * 2 + (1 - core))
    early, late = z1 == 0, z1 == 1
    early_0, early_1 = jnp.logical_and(early, core == 0), jnp.logical_and(early, core == 1)
    late_0, late_1 = jnp.logical_and(late, core == 0), jnp.logical_and(late, core == 1)
    takes = 1 - flip(x // 2, lax.rem(x, 2))
    pair = (dp, (x + 1 - 2 * lax.rem(x, 2)) * 4 + z_lo * 2 + core)
    crosses = jnp.logical_and(core == 1, z0 == takes)

    def at(y, z_hi, lo, to_core):
        return (y * 4 + z_hi, x * 4 + lo * 2 + to_core)

    def within(half):
        return [at(y, half * 2 + z, z_lo, 0) for z in range(2) for y in SERVE_Y]

    def across(half, to_core):
        return [at(y, half * 2 + z, flip(z_lo, flip(z0, z + 1)), to_core) for z in range(2) for y in SERVE_Y]

    def crossing_to_here(half, from_core):
        return [at(y, half * 2 + takes, flip(z_lo, flip(z0, takes + 1)), from_core) for y in SERVE_Y]

    def load(i):
        src, dst = (
            (lora_in_hbm, lora_in), (lora_out_hbm, lora_out), (hidden_hbm, hidden), (base_hbm, base),
            (keys_hbm, keys), (values_hbm, values), (gain_hbm, gain), (lengths_hbm, lengths),
        )[i]
        return pltpu.make_async_copy(src, dst, in_sems.at[i])

    for i in (0, 1):
        load(i).start()

    barrier = pltpu.get_barrier_semaphore()

    def signal(device):
        pl.semaphore_signal(barrier, inc=1, device_id=device, device_id_type=MESH)

    @pl.when(core == 0)
    def _():
        for device in within(z1):
            @pl.when(device[0] != dp)
            def _():
                signal(device)

    @pl.when(late_0)
    def _():
        for device in crossing_to_here(0, 1):
            signal(device)
        signal(pair)

    @pl.when(early_1)
    def _():
        for device in crossing_to_here(1, 1):
            signal(device)
        signal(pair)

    @pl.when(jnp.logical_not(late_0))
    def _():
        signal(sibling)

    @pl.when(early)
    def _():
        for i in range(2, 8):
            load(i).start()

    load(0).wait()
    load(1).wait()
    rows = jnp.transpose(lora_in[...].astype(jnp.float32))
    packed = jnp.concatenate([rows[:PACKED], rows[PACKED:]], axis=1)
    slots[dp] = packed.astype(jnp.bfloat16)
    x_pair = x // 2 * 2
    for lo in range(2):
        columns = []
        for k in range(2):
            even = lora_out[(x_pair + k) * 4 + lo * 2].astype(jnp.float32)
            odd = lora_out[(x_pair + k) * 4 + lo * 2 + 1].astype(jnp.float32)
            columns.append(jnp.concatenate([even, odd], axis=1))
        own_ups[lo] = jnp.concatenate(columns, axis=0).astype(jnp.bfloat16)
    ups[dp] = own_ups[z_lo]

    def prepare():
        for i in range(4, 8):
            load(i).wait()
        square = (32, 128)
        on_diagonal = lax.broadcasted_iota(jnp.int32, square, 0) == lax.broadcasted_iota(jnp.int32, square, 1)
        length_row = jnp.concatenate([lengths[...], jnp.zeros((1, 96), jnp.int32)], axis=1).astype(jnp.float32)
        length_column = jnp.sum(jnp.where(on_diagonal, length_row, 0.0), axis=1, keepdims=True).astype(jnp.int32)
        tile = (16, 512)
        row = lax.rem(lax.broadcasted_iota(jnp.int32, tile, 0), 8)
        column = lax.broadcasted_iota(jnp.int32, tile, 1)
        own_row = column // 64 == row
        position = lax.rem(column, 64)
        for j in range(4):
            length = jnp.concatenate([length_column[j * 8:j * 8 + 8]] * 2, axis=0)
            bias[j] = jnp.where(jnp.logical_and(own_row, position < length), 0.0, -jnp.inf)
            turned_keys[j] = jnp.transpose(keys[j * 8:j * 8 + 8].reshape(512, 128))
        load(2).wait()
        for c in range(4):
            pieces = [hidden[:, s * 160:s * 160 + 160].astype(jnp.float32) for s in chunk(c // 2, c % 2)]
            ordered[c] = jnp.concatenate(pieces, axis=1).astype(jnp.bfloat16)
        load(3).wait()

    @pl.when(early)
    def _():
        prepare()

    @pl.when(jnp.logical_or(jnp.logical_not(late_1), crosses))
    def _():
        pl.semaphore_wait(barrier, jnp.where(early_1, jnp.where(crosses, 18, 2), jnp.where(late_0, 17, 16)))

    def remote(src, dst, send_sem, recv_sem, device):
        return pltpu.make_async_remote_copy(
            src_ref=src, dst_ref=dst, send_sem=send_sem, recv_sem=recv_sem, device_id=device, device_id_type=MESH
        )

    def down(s, send_sem, device):
        return remote(slots.at[s], slots.at[s], send_sem.at[0], recv.at[0, s], device)

    def up(s, send_sem, device):
        return remote(ups.at[s], ups.at[s], send_sem.at[1], recv.at[1, s], device)

    def own_up(send_sem, device):
        z_lo_there = lax.rem(device[1] // 2, 2)
        return remote(own_ups.at[z_lo_there], ups.at[dp], send_sem.at[1], recv.at[1, dp], device)

    def own_down(send_sem, device):
        return down(dp, send_sem, device)

    def serve(act):
        @pl.when(jnp.logical_and(late, crosses))
        def _():
            for i, device in enumerate(across(0, 1)):
                act(send_dp.at[i], device)

        @pl.when(jnp.logical_and(early, crosses))
        def _():
            for i, device in enumerate(across(1, 0)):
                act(send_dp.at[i], device)

        @pl.when(core == 0)
        def _():
            for i, device in enumerate(within(z1)):
                @pl.when(device[0] != dp)
                def _():
                    act(send_dp.at[i], device)

    serve(lambda sem, device: own_up(sem, device).start())
    serve(lambda sem, device: own_down(sem, device).start())

    @pl.when(late)
    def _():
        for i in range(2, 8):
            load(i).start()

    def half_shards(half):
        return chunk(half, 0) + chunk(half, 1)

    def arrive(kind, s):
        kind(s, send_core.at[0], sibling).wait_recv()

    def forward_own(kind, act):
        @pl.when(core == 0)
        def _():
            for i, s in enumerate(half_shards(z1)):
                @pl.when(s != dp)
                def _():
                    act(kind, s, i)

    def forward_other(kind, act, s, i):
        @pl.when(late_0)
        def _():
            act(kind, s, 16 + i)

        @pl.when(early_1)
        def _():
            act(kind, s, i)

        @pl.when(jnp.logical_and(jnp.logical_or(late_0, early_1), i // 8 == takes))
        def _():
            act(kind, s, i, True)

    def pass_on(kind, s, i, to_pair=False):
        if to_pair:
            kind(s, send_pair.at[i % 8], pair).start()
        else:
            arrive(kind, s)
            kind(s, send_core.at[i], sibling).start()

    others = half_shards(1 - z1)
    forward_own(up, pass_on)
    forward_own(down, pass_on)

    @pl.when(late)
    def _():
        prepare()

    def forward_others(kind, places):
        for i in places:
            forward_other(kind, pass_on, others[i], i)

    def own_from_sibling(kind):
        @pl.when(core == 1)
        def _():
            for s in half_shards(z1):
                @pl.when(s != dp)
                def _():
                    arrive(kind, s)

    def others_from_sibling(kind, places):
        @pl.when(jnp.logical_or(early_0, late_1))
        def _():
            for i in places:
                arrive(kind, others[i])

    z_0, z_1 = range(8), range(8, 16)
    forward_others(up, z_0)
    forward_others(down, z_0)
    forward_others(up, z_1)
    own_from_sibling(up)
    own_from_sibling(down)
    others_from_sibling(up, z_0)
    others_from_sibling(up, z_1)

    lows = ups[...].astype(jnp.float32)
    both = jnp.where(lax.rem(x, 2) == 0, lows[:, :8], lows[:, 8:]).reshape(256, 128)
    turned = pltpu.roll(both, 64, 1)
    lane = lax.broadcasted_iota(jnp.int32, (128, 256), 0)
    first = jnp.transpose(jnp.where(core == 0, both, turned))
    second = jnp.transpose(jnp.where(core == 0, turned, both))
    spread[:, :256] = jnp.where(lane < 64, first, 0.0).astype(jnp.bfloat16)
    spread[:, 256:] = jnp.where(lane >= 64, second, 0.0).astype(jnp.bfloat16)

    def project(half, z):
        at = half * 2 + z
        for k, s in enumerate(chunk(half, z)):
            update = jnp.dot(slots[s], spread[...], preferred_element_type=jnp.float32)
            for part in range(2):
                rows = pl.ds(pl.multiple_of(s * 160 + part * PACKED, 16), PACKED)
                total = base[rows, :].astype(jnp.float32) + update[:, part * 256:part * 256 + 256]
                merged[at, k * 160 + part * PACKED:k * 160 + part * PACKED + PACKED] = total.astype(jnp.bfloat16)
        return jnp.dot(ordered[at], merged[at], preferred_element_type=jnp.float32)

    query = project(z1, 0) + project(z1, 1)
    forward_others(down, z_1)
    others_from_sibling(down, z_0)
    query += project(1 - z1, 0)
    others_from_sibling(down, z_1)
    query += project(1 - z1, 1)

    gains = gain[...]
    heads = []
    for h in range(2):
        head = query[:, h * 128:h * 128 + 128]
        inverse = lax.rsqrt(jnp.mean(head * head, axis=-1, keepdims=True) + 1e-06)
        heads.append(head * inverse * gains)
    parts = []
    for j in range(4):
        normed = jnp.concatenate([heads[0][j * 8:j * 8 + 8], heads[1][j * 8:j * 8 + 8]], axis=0).astype(jnp.bfloat16)
        values_tile = values[j * 8:j * 8 + 8].reshape(512, 128)
        scores = jnp.dot(normed, turned_keys[j], preferred_element_type=jnp.float32) / math.sqrt(128) + bias[j]
        expo = jnp.exp(scores - jnp.max(scores, axis=-1, keepdims=True))
        weights = (expo * (1.0 / jnp.sum(expo, axis=-1, keepdims=True))).astype(jnp.bfloat16)
        parts.append(jnp.dot(weights, values_tile, preferred_element_type=jnp.float32))
    out_ref[...] = jnp.concatenate(
        [jnp.concatenate([part[h * 8:h * 8 + 8] for part in parts], axis=0) for h in range(2)], axis=1
    ).astype(jnp.bfloat16)

    serve(lambda sem, device: own_up(sem, device).wait_send())
    serve(lambda sem, device: own_down(sem, device).wait_send())

    def sent(kind, s, i, to_pair=False):
        if to_pair:
            kind(s, send_pair.at[i % 8], pair).wait_send()
        else:
            kind(s, send_core.at[i], sibling).wait_send()

    for kind in (up, down):
        forward_own(kind, sent)
        for i, s in enumerate(others):
            forward_other(kind, sent, s, i)


def local(
    hidden, query_base_matrix, input_side_factor, output_side_factor,
    query_norm_gain, cached_key_heads, cached_value_heads, lengths,
):
    bf16 = jnp.bfloat16
    return pl.pallas_call(
        kernel,
        out_shape=jax.ShapeDtypeStruct((32, 256), bf16),
        in_specs=[pl.BlockSpec(memory_space=pl.ANY)] * 8,
        out_specs=pl.BlockSpec(memory_space=pltpu.VMEM),
        scratch_shapes=[
            pltpu.VMEM((32, 5120), bf16),
            pltpu.VMEM((5120, 256), bf16),
            pltpu.VMEM((64, 160), bf16),
            pltpu.VMEM((16, 8, 64), bf16),
            pltpu.VMEM((1, 128), jnp.float32),
            pltpu.VMEM((32, 64, 128), bf16),
            pltpu.VMEM((32, 64, 128), bf16),
            pltpu.VMEM((1, 32), jnp.int32),
            pltpu.VMEM((N_DP, PACKED, 128), bf16),
            pltpu.VMEM((N_DP, GROUP, 128), bf16),
            pltpu.VMEM((2, GROUP, 128), bf16),
            pltpu.VMEM((128, 512), bf16),
            pltpu.VMEM((4, 1280, 256), bf16),
            pltpu.VMEM((4, 32, 1280), bf16),
            pltpu.VMEM((4, 128, 512), bf16),
            pltpu.VMEM((4, 16, 512), jnp.float32),
            pltpu.SemaphoreType.DMA((8,)),
            pltpu.SemaphoreType.DMA((16, 2)),
            pltpu.SemaphoreType.DMA((8, 2)),
            pltpu.SemaphoreType.DMA((32, 2)),
            pltpu.SemaphoreType.DMA((2, N_DP)),
        ],
        compiler_params=pltpu.CompilerParams(
            collective_id=0, has_side_effects=True, vmem_limit_bytes=56 * 2**20
        ),
        cost_estimate=pl.CostEstimate(flops=260_000_000, bytes_accessed=4_200_000, transcendentals=32768),
    )(
        hidden, query_base_matrix, input_side_factor.T, jnp.transpose(output_side_factor, (1, 2, 0)),
        query_norm_gain.reshape(1, 128), cached_key_heads.reshape(32, 64, 128),
        cached_value_heads.reshape(32, 64, 128), lengths.reshape(1, 32),
    )


def solution(mesh):
    in_specs = (
        P("dp", None),
        P(None, "tensor"),
        P("dp", None),
        P(None, None, "dp"),
        P(),
        P("dp", "tensor", None, None),
        P("dp", "tensor", None, None),
        P("dp"),
    )
    return jax.shard_map(local, mesh=mesh, in_specs=in_specs, out_specs=P("dp", "tensor"), check_vma=False)
```

```python
import functools
import math

import jax
import jax.numpy as jnp
from jax import lax
from jax.experimental import pallas as pl
from jax.experimental.pallas import tpu as pltpu
from jax.sharding import PartitionSpec as P

MESH = pl.DeviceIdType.MESH
N_DP = 32
PACKED = 80
GROUP = 16
SERVE_Y = (0, 1, 2, 3, 7, 6, 5, 4)
AWAIT_Y = (0, 1, 7, 2, 6, 3, 5, 4)


def flip(bit, other):
    return lax.rem(bit + other, 2)


def chunk(half, z):
    return [y * 4 + half * 2 + z for y in AWAIT_Y]


def kernel(
    hidden_hbm, base_hbm, lora_in_hbm, lora_out_hbm, gain_hbm, keys_hbm, values_hbm, lengths_hbm,
    out_ref,
    hidden, base, lora_in, lora_out, gain, keys, values, lengths,
    slots, ups, own_ups, spread, merged, ordered, turned_keys, bias,
    in_sems, send_dp, send_pair, send_core, recv, recv_core,
):
    dp, t = lax.axis_index("dp"), lax.axis_index("tensor")
    x, z_lo, core = t // 4, lax.rem(t // 2, 2), lax.rem(t, 2)
    z1, z0 = lax.rem(dp // 2, 2), lax.rem(dp, 2)
    sibling = (dp, x * 4 + z_lo * 2 + (1 - core))
    early, late = z1 == 0, z1 == 1
    early_0, early_1 = jnp.logical_and(early, core == 0), jnp.logical_and(early, core == 1)
    late_0, late_1 = jnp.logical_and(late, core == 0), jnp.logical_and(late, core == 1)
    takes = 1 - flip(x // 2, lax.rem(x, 2))
    pair = (dp, (x + 1 - 2 * lax.rem(x, 2)) * 4 + z_lo * 2 + core)
    crosses = jnp.logical_and(core == 1, z0 == takes)

    def at(y, z_hi, lo, to_core):
        return (y * 4 + z_hi, x * 4 + lo * 2 + to_core)

    def within(half):
        return [at(y, half * 2 + z, z_lo, 0) for z in range(2) for y in SERVE_Y]

    def across(half, to_core):
        return [at(y, half * 2 + z, flip(z_lo, flip(z0, z + 1)), to_core) for z in range(2) for y in SERVE_Y]

    def crossing_to_here(half, from_core):
        return [at(y, half * 2 + takes, flip(z_lo, flip(z0, takes + 1)), from_core) for y in SERVE_Y]

    def load(i):
        src, dst = (
            (lora_in_hbm, lora_in), (lora_out_hbm, lora_out), (hidden_hbm, hidden), (base_hbm, base),
            (keys_hbm, keys), (values_hbm, values), (gain_hbm, gain), (lengths_hbm, lengths),
        )[i]
        return pltpu.make_async_copy(src, dst, in_sems.at[i])

    for i in (0, 1):
        load(i).start()

    barrier = pltpu.get_barrier_semaphore()

    def signal(device):
        pl.semaphore_signal(barrier, inc=1, device_id=device, device_id_type=MESH)

    @pl.when(core == 0)
    def _():
        for device in within(z1):
            @pl.when(device[0] != dp)
            def _():
                signal(device)

    @pl.when(late_0)
    def _():
        for device in across(0, 1):
            signal(device)

    @pl.when(early_1)
    def _():
        for device in crossing_to_here(1, 1):
            signal(device)
        signal(pair)

    @pl.when(jnp.logical_not(late_0))
    def _():
        signal(sibling)

    @pl.when(early)
    def _():
        for i in range(2, 8):
            load(i).start()

    load(0).wait()
    load(1).wait()
    rows = jnp.transpose(lora_in[...].astype(jnp.float32))
    packed = jnp.concatenate([rows[:PACKED], rows[PACKED:]], axis=1)
    slots[dp] = packed.astype(jnp.bfloat16)
    x_pair = x // 2 * 2
    for lo in range(2):
        columns = []
        for k in range(2):
            even = lora_out[(x_pair + k) * 4 + lo * 2].astype(jnp.float32)
            odd = lora_out[(x_pair + k) * 4 + lo * 2 + 1].astype(jnp.float32)
            columns.append(jnp.concatenate([even, odd], axis=1))
        own_ups[lo] = jnp.concatenate(columns, axis=0).astype(jnp.bfloat16)
    ups[dp] = own_ups[z_lo]

    def prepare():
        for i in range(4, 8):
            load(i).wait()
        square = (32, 128)
        on_diagonal = lax.broadcasted_iota(jnp.int32, square, 0) == lax.broadcasted_iota(jnp.int32, square, 1)
        length_row = jnp.concatenate([lengths[...], jnp.zeros((1, 96), jnp.int32)], axis=1).astype(jnp.float32)
        length_column = jnp.sum(jnp.where(on_diagonal, length_row, 0.0), axis=1, keepdims=True).astype(jnp.int32)
        tile = (16, 512)
        row = lax.rem(lax.broadcasted_iota(jnp.int32, tile, 0), 8)
        column = lax.broadcasted_iota(jnp.int32, tile, 1)
        own_row = column // 64 == row
        position = lax.rem(column, 64)
        for j in range(4):
            length = jnp.concatenate([length_column[j * 8:j * 8 + 8]] * 2, axis=0)
            bias[j] = jnp.where(jnp.logical_and(own_row, position < length), 0.0, -jnp.inf)
            turned_keys[j] = jnp.transpose(keys[j * 8:j * 8 + 8].reshape(512, 128))
        load(2).wait()
        for c in range(4):
            pieces = [hidden[:, s * 160:s * 160 + 160].astype(jnp.float32) for s in chunk(c // 2, c % 2)]
            ordered[c] = jnp.concatenate(pieces, axis=1).astype(jnp.bfloat16)
        load(3).wait()

    @pl.when(early)
    def _():
        prepare()

    @pl.when(jnp.logical_or(jnp.logical_not(late_1), crosses))
    def _():
        pl.semaphore_wait(barrier, jnp.where(early_1, 18, 16))

    def remote(src, dst, send_sem, recv_sem, device):
        return pltpu.make_async_remote_copy(
            src_ref=src, dst_ref=dst, send_sem=send_sem, recv_sem=recv_sem, device_id=device, device_id_type=MESH
        )

    def down(s, send_sem, recv_sem, device):
        return remote(slots.at[s], slots.at[s], send_sem.at[0], recv_sem.at[0], device)

    def up(s, send_sem, recv_sem, device):
        return remote(ups.at[s], ups.at[s], send_sem.at[1], recv_sem.at[1], device)

    def own_up(device):
        z_lo_there = lax.rem(device[1] // 2, 2)
        return remote(own_ups.at[z_lo_there], ups.at[dp], send_dp.at[1], recv.at[dp, 1], device)

    def own_down(device):
        return down(dp, send_dp, recv.at[dp], device)

    def many(kind, n, send_sem, recv_sem):
        ref, at = (slots, 0) if kind is down else (ups, 1)
        return remote(ref.at[pl.ds(0, n)], ref.at[pl.ds(0, n)], send_sem.at[at], recv_sem.at[at], sibling)

    def serve(act):
        @pl.when(jnp.logical_and(late, crosses))
        def _():
            for device in across(0, 1):
                act(device)

        @pl.when(early_1)
        def _():
            for device in across(1, 0):
                act(device)

        @pl.when(core == 0)
        def _():
            for device in within(z1):
                @pl.when(device[0] != dp)
                def _():
                    act(device)

    serve(lambda device: own_up(device).start())
    serve(lambda device: own_down(device).start())

    @pl.when(late)
    def _():
        for i in range(2, 8):
            load(i).start()

    def half_shards(half):
        return chunk(half, 0) + chunk(half, 1)

    def pass_on(kind, s, group):
        kind(s, send_core, recv.at[s], sibling).wait_recv()
        kind(s, send_core, recv_core.at[group], sibling).start()

    def pass_own(kind):
        @pl.when(core == 0)
        def _():
            for s in half_shards(z1):
                @pl.when(s != dp)
                def _():
                    pass_on(kind, s, 0)

    others = chunk(1 - z1, takes) + chunk(1 - z1, 1 - takes)

    def pass_straight(kind, role):
        @pl.when(role)
        def _():
            for s in others[:8]:
                pass_on(kind, s, 1)

                @pl.when(early)
                def _():
                    kind(s, send_pair, recv.at[s], pair).start()

    def pass_rest(kind):
        @pl.when(jnp.logical_or(late_0, early_1))
        def _():
            for i, s in enumerate(others[8:]):
                pass_on(kind, s, 2 + i // 4)

    def from_sibling(kind, group):
        role = core == 1 if group == 0 else jnp.logical_or(early_0, late_1)

        @pl.when(role)
        def _():
            many(kind, (15, 8, 4, 4)[group], send_core, recv_core.at[group]).wait_recv()

    pass_own(up)
    pass_own(down)

    @pl.when(late)
    def _():
        prepare()

    pass_straight(up, jnp.logical_or(late_0, early_1))
    pass_straight(down, early_1)
    pass_rest(up)
    from_sibling(up, 0)
    from_sibling(down, 0)
    from_sibling(up, 1)
    from_sibling(up, 2)
    from_sibling(up, 3)

    lows = ups[...].astype(jnp.float32)
    both = jnp.where(lax.rem(x, 2) == 0, lows[:, :8], lows[:, 8:]).reshape(256, 128)
    turned = pltpu.roll(both, 64, 1)
    lane = lax.broadcasted_iota(jnp.int32, (128, 256), 0)
    first = jnp.transpose(jnp.where(core == 0, both, turned))
    second = jnp.transpose(jnp.where(core == 0, turned, both))
    spread[:, :256] = jnp.where(lane < 64, first, 0.0).astype(jnp.bfloat16)
    spread[:, 256:] = jnp.where(lane >= 64, second, 0.0).astype(jnp.bfloat16)

    def project(half, z, places=(0, 8)):
        at = half * 2 + z
        begin, end = places
        for k, s in enumerate(chunk(half, z)):
            if not begin <= k < end:
                continue
            update = jnp.dot(slots[s], spread[...], preferred_element_type=jnp.float32)
            for part in range(2):
                rows = pl.ds(pl.multiple_of(s * 160 + part * PACKED, 16), PACKED)
                total = base[rows, :].astype(jnp.float32) + update[:, part * 256:part * 256 + 256]
                merged[at, k * 160 + part * PACKED:k * 160 + part * PACKED + PACKED] = total.astype(jnp.bfloat16)
        columns = slice(begin * 160, end * 160)
        return jnp.dot(ordered[at, :, columns], merged[at, columns], preferred_element_type=jnp.float32)

    query = project(z1, 0) + project(z1, 1)
    pass_straight(down, late_0)
    pass_rest(down)
    from_sibling(down, 1)
    query += project(1 - z1, takes)
    from_sibling(down, 2)
    query += project(1 - z1, 1 - takes, (0, 4))
    from_sibling(down, 3)
    query += project(1 - z1, 1 - takes, (4, 8))

    gains = gain[...]
    heads = []
    for h in range(2):
        head = query[:, h * 128:h * 128 + 128]
        inverse = lax.rsqrt(jnp.mean(head * head, axis=-1, keepdims=True) + 1e-06)
        heads.append(head * inverse * gains)
    parts = []
    for j in range(4):
        normed = jnp.concatenate([heads[0][j * 8:j * 8 + 8], heads[1][j * 8:j * 8 + 8]], axis=0).astype(jnp.bfloat16)
        values_tile = values[j * 8:j * 8 + 8].reshape(512, 128)
        scores = jnp.dot(normed, turned_keys[j], preferred_element_type=jnp.float32) * (1.0 / math.sqrt(128)) + bias[j]
        expo = jnp.exp(scores - jnp.max(scores, axis=-1, keepdims=True))
        weights = (expo * (1.0 / jnp.sum(expo, axis=-1, keepdims=True))).astype(jnp.bfloat16)
        parts.append(jnp.dot(weights, values_tile, preferred_element_type=jnp.float32))
    out_ref[...] = jnp.concatenate(
        [jnp.concatenate([part[h * 8:h * 8 + 8] for part in parts], axis=0) for h in range(2)], axis=1
    ).astype(jnp.bfloat16)

    def sent(n, sem):
        for kind in (up, down):
            many(kind, n, sem, recv_core.at[0]).wait_send()

    @pl.when(core == 0)
    def _():
        sent(15, send_dp)

    @pl.when(early_0)
    def _():
        sent(15, send_core)

    @pl.when(late_0)
    def _():
        sent(31, send_core)

    @pl.when(early_1)
    def _():
        sent(16, send_dp)
        sent(16, send_core)
        sent(8, send_pair)

    @pl.when(jnp.logical_and(late, crosses))
    def _():
        sent(16, send_dp)


def local(
    hidden, query_base_matrix, input_side_factor, output_side_factor,
    query_norm_gain, cached_key_heads, cached_value_heads, lengths,
):
    bf16 = jnp.bfloat16
    return pl.pallas_call(
        kernel,
        out_shape=jax.ShapeDtypeStruct((32, 256), bf16),
        in_specs=[pl.BlockSpec(memory_space=pltpu.HBM)] * 8,
        out_specs=pl.BlockSpec(memory_space=pltpu.VMEM),
        scratch_shapes=[
            pltpu.VMEM((32, 5120), bf16),
            pltpu.VMEM((5120, 256), bf16),
            pltpu.VMEM((64, 160), bf16),
            pltpu.VMEM((16, 8, 64), bf16),
            pltpu.VMEM((1, 128), jnp.float32),
            pltpu.VMEM((32, 64, 128), bf16),
            pltpu.VMEM((32, 64, 128), bf16),
            pltpu.VMEM((1, 32), jnp.int32),
            pltpu.VMEM((N_DP, PACKED, 128), bf16),
            pltpu.VMEM((N_DP, GROUP, 128), bf16),
            pltpu.VMEM((2, GROUP, 128), bf16),
            pltpu.VMEM((128, 512), bf16),
            pltpu.VMEM((4, 1280, 256), bf16),
            pltpu.VMEM((4, 32, 1280), bf16),
            pltpu.VMEM((4, 128, 512), bf16),
            pltpu.VMEM((4, 16, 512), jnp.float32),
            pltpu.SemaphoreType.DMA((8,)),
            pltpu.SemaphoreType.DMA((2,)),
            pltpu.SemaphoreType.DMA((2,)),
            pltpu.SemaphoreType.DMA((2,)),
            pltpu.SemaphoreType.DMA((N_DP, 2)),
            pltpu.SemaphoreType.DMA((4, 2)),
        ],
        compiler_params=pltpu.CompilerParams(
            collective_id=0, has_side_effects=True, vmem_limit_bytes=56 * 2**20
        ),
        cost_estimate=pl.CostEstimate(flops=260_000_000, bytes_accessed=4_200_000, transcendentals=32768),
    )(
        hidden, query_base_matrix, input_side_factor.T, jnp.transpose(output_side_factor, (1, 2, 0)),
        query_norm_gain.reshape(1, 128), cached_key_heads.reshape(32, 64, 128),
        cached_value_heads.reshape(32, 64, 128), lengths.reshape(1, 32),
    )


def solution(mesh):
    in_specs = (
        P("dp", None),
        P(None, "tensor"),
        P("dp", None),
        P(None, None, "dp"),
        P(),
        P("dp", "tensor", None, None),
        P("dp", "tensor", None, None),
        P("dp"),
    )
    return jax.shard_map(local, mesh=mesh, in_specs=in_specs, out_specs=P("dp", "tensor"), check_vma=False)
```

```python
import functools
import math

import jax
import jax.numpy as jnp
from jax import lax
from jax.experimental import pallas as pl
from jax.experimental.pallas import tpu as pltpu
from jax.sharding import PartitionSpec as P

MESH = pl.DeviceIdType.MESH
N_DP = 32
PACKED = 80
GROUP = 16
SERVE_Y = (0, 1, 2, 3, 7, 6, 5, 4)
AWAIT_Y = (0, 1, 7, 2, 6, 3, 5, 4)


def flip(bit, other):
    return lax.rem(bit + other, 2)


def chunk(half, z):
    return [y * 4 + half * 2 + z for y in AWAIT_Y]


def kernel(
    hidden_hbm, base_hbm, lora_in_hbm, lora_out_hbm, gain_hbm, keys_hbm, values_hbm, lengths_hbm,
    out_ref,
    hidden, base, lora_in, lora_out, gain, keys, values, lengths,
    slots, ups, own_ups, spread, merged, ordered, turned_keys, bias,
    in_sems, send_dp, send_pair, send_core, recv, recv_core,
):
    dp, t = lax.axis_index("dp"), lax.axis_index("tensor")
    x, z_lo, core = t // 4, lax.rem(t // 2, 2), lax.rem(t, 2)
    z1, z0 = lax.rem(dp // 2, 2), lax.rem(dp, 2)
    sibling = (dp, x * 4 + z_lo * 2 + (1 - core))
    early, late = z1 == 0, z1 == 1
    early_0, early_1 = jnp.logical_and(early, core == 0), jnp.logical_and(early, core == 1)
    late_0, late_1 = jnp.logical_and(late, core == 0), jnp.logical_and(late, core == 1)
    takes = 1 - flip(x // 2, lax.rem(x, 2))
    pair = (dp, (x + 1 - 2 * lax.rem(x, 2)) * 4 + z_lo * 2 + core)
    crosses = jnp.logical_and(core == 1, z0 == takes)

    def at(y, z_hi, lo, to_core):
        return (y * 4 + z_hi, x * 4 + lo * 2 + to_core)

    def within(half):
        return [at(y, half * 2 + z, z_lo, 0) for z in range(2) for y in SERVE_Y]

    def across(half, to_core):
        return [at(y, half * 2 + z, flip(z_lo, flip(z0, z + 1)), to_core) for z in range(2) for y in SERVE_Y]

    to_late = [at(y, 2 + z_lo, lo, 0) for lo in range(2) for y in SERVE_Y]
    from_early = [at(y, z, z0, 1) for z in range(2) for y in SERVE_Y]

    def crossing_to_here(half, from_core):
        return [at(y, half * 2 + takes, flip(z_lo, flip(z0, takes + 1)), from_core) for y in SERVE_Y]

    def load(i):
        src, dst = (
            (lora_in_hbm, lora_in), (lora_out_hbm, lora_out), (hidden_hbm, hidden), (base_hbm, base),
            (keys_hbm, keys), (values_hbm, values), (gain_hbm, gain), (lengths_hbm, lengths),
        )[i]
        return pltpu.make_async_copy(src, dst, in_sems.at[i])

    for i in (0, 1):
        load(i).start()

    barrier = pltpu.get_barrier_semaphore()

    def signal(device):
        pl.semaphore_signal(barrier, inc=1, device_id=device, device_id_type=MESH)

    @pl.when(late_0)
    def _():
        for device in from_early:
            signal(device)

    @pl.when(core == 0)
    def _():
        for device in within(z1):
            @pl.when(device[0] != dp)
            def _():
                signal(device)

    @pl.when(early_1)
    def _():
        for device in crossing_to_here(1, 1):
            signal(device)
        signal(pair)

    @pl.when(jnp.logical_not(late_0))
    def _():
        signal(sibling)

    @pl.when(early)
    def _():
        for i in range(2, 8):
            load(i).start()

    load(1).wait()
    x_pair = x // 2 * 2
    for lo in range(2):
        columns = []
        for k in range(2):
            even = lora_out[(x_pair + k) * 4 + lo * 2].astype(jnp.float32)
            odd = lora_out[(x_pair + k) * 4 + lo * 2 + 1].astype(jnp.float32)
            columns.append(jnp.concatenate([even, odd], axis=1))
        own_ups[lo] = jnp.concatenate(columns, axis=0).astype(jnp.bfloat16)
    ups[dp] = own_ups[z_lo]

    def prepare():
        for i in range(4, 8):
            load(i).wait()
        square = (32, 128)
        on_diagonal = lax.broadcasted_iota(jnp.int32, square, 0) == lax.broadcasted_iota(jnp.int32, square, 1)
        length_row = jnp.concatenate([lengths[...], jnp.zeros((1, 96), jnp.int32)], axis=1).astype(jnp.float32)
        length_column = jnp.sum(jnp.where(on_diagonal, length_row, 0.0), axis=1, keepdims=True).astype(jnp.int32)
        tile = (16, 512)
        row = lax.rem(lax.broadcasted_iota(jnp.int32, tile, 0), 8)
        column = lax.broadcasted_iota(jnp.int32, tile, 1)
        own_row = column // 64 == row
        position = lax.rem(column, 64)
        for j in range(4):
            length = jnp.concatenate([length_column[j * 8:j * 8 + 8]] * 2, axis=0)
            bias[j] = jnp.where(jnp.logical_and(own_row, position < length), 0.0, -jnp.inf)
            turned_keys[j] = jnp.transpose(keys[j * 8:j * 8 + 8].reshape(512, 128))
        load(2).wait()
        for c in range(4):
            pieces = [hidden[:, s * 160:s * 160 + 160].astype(jnp.float32) for s in chunk(c // 2, c % 2)]
            ordered[c] = jnp.concatenate(pieces, axis=1).astype(jnp.bfloat16)
        load(3).wait()

    @pl.when(early)
    def _():
        prepare()

    @pl.when(jnp.logical_or(jnp.logical_not(late_1), crosses))
    def _():
        pl.semaphore_wait(barrier, jnp.where(early_1, 18, 16))

    def remote(src, dst, send_sem, recv_sem, device):
        return pltpu.make_async_remote_copy(
            src_ref=src, dst_ref=dst, send_sem=send_sem, recv_sem=recv_sem, device_id=device, device_id_type=MESH
        )

    def down(s, send_sem, recv_sem, device):
        return remote(slots.at[s], slots.at[s], send_sem.at[0], recv_sem.at[0], device)

    def up(s, send_sem, recv_sem, device):
        return remote(ups.at[s], ups.at[s], send_sem.at[1], recv_sem.at[1], device)

    def own_up(device):
        z_lo_there = lax.rem(device[1] // 2, 2)
        return remote(own_ups.at[z_lo_there], ups.at[dp], send_dp.at[1], recv.at[dp, 1], device)

    def own_down(device):
        return down(dp, send_dp, recv.at[dp], device)

    def many(kind, n, send_sem, recv_sem):
        ref, at = (slots, 0) if kind is down else (ups, 1)
        return remote(ref.at[pl.ds(0, n)], ref.at[pl.ds(0, n)], send_sem.at[at], recv_sem.at[at], sibling)

    def serve(act):
        @pl.when(jnp.logical_and(late, crosses))
        def _():
            for device in across(0, 1):
                act(device)

        @pl.when(early_1)
        def _():
            for device in to_late:
                act(device)

        @pl.when(core == 0)
        def _():
            for device in within(z1):
                @pl.when(device[0] != dp)
                def _():
                    act(device)

    serve(lambda device: own_up(device).start())

    load(0).wait()
    rows = jnp.transpose(lora_in[...].astype(jnp.float32))
    packed = jnp.concatenate([rows[:PACKED], rows[PACKED:]], axis=1)
    slots[dp] = packed.astype(jnp.bfloat16)

    serve(lambda device: own_down(device).start())

    @pl.when(late)
    def _():
        for i in range(2, 8):
            load(i).start()

    def half_shards(half):
        return chunk(half, 0) + chunk(half, 1)

    def pass_on(kind, s, group):
        kind(s, send_core, recv.at[s], sibling).wait_recv()
        kind(s, send_core, recv_core.at[group], sibling).start()

    def pass_own(kind):
        @pl.when(core == 0)
        def _():
            for s in half_shards(z1):
                @pl.when(s != dp)
                def _():
                    pass_on(kind, s, 0)

    others = chunk(1 - z1, takes) + chunk(1 - z1, 1 - takes)

    def pass_straight(kind, role):
        @pl.when(role)
        def _():
            for s in others[:8]:
                pass_on(kind, s, 1)

                @pl.when(early)
                def _():
                    kind(s, send_pair, recv.at[s], pair).start()

    def pass_rest(kind, groups=(2, 3)):
        @pl.when(jnp.logical_or(late_0, early_1))
        def _():
            for group in groups:
                for s in others[group * 4:group * 4 + 4]:
                    pass_on(kind, s, group)

    def from_sibling(kind, group):
        role = core == 1 if group == 0 else jnp.logical_or(early_0, late_1)

        @pl.when(role)
        def _():
            many(kind, (15, 8, 4, 4)[group], send_core, recv_core.at[group]).wait_recv()

    pass_own(up)
    pass_own(down)

    @pl.when(late)
    def _():
        prepare()

    pass_straight(up, jnp.logical_or(late_0, early_1))
    pass_straight(down, early_1)
    pass_rest(up)
    from_sibling(up, 0)
    from_sibling(down, 0)
    from_sibling(up, 1)
    from_sibling(up, 2)
    from_sibling(up, 3)

    lows = ups[...].astype(jnp.float32)
    both = jnp.where(lax.rem(x, 2) == 0, lows[:, :8], lows[:, 8:]).reshape(256, 128)
    turned = pltpu.roll(both, 64, 1)
    lane = lax.broadcasted_iota(jnp.int32, (128, 256), 0)
    first = jnp.transpose(jnp.where(core == 0, both, turned))
    second = jnp.transpose(jnp.where(core == 0, turned, both))
    spread[:, :256] = jnp.where(lane < 64, first, 0.0).astype(jnp.bfloat16)
    spread[:, 256:] = jnp.where(lane >= 64, second, 0.0).astype(jnp.bfloat16)

    def project(half, z, places=(0, 8)):
        at = half * 2 + z
        begin, end = places
        for k, s in enumerate(chunk(half, z)):
            if not begin <= k < end:
                continue
            update = jnp.dot(slots[s], spread[...], preferred_element_type=jnp.float32)
            for part in range(2):
                rows = pl.ds(pl.multiple_of(s * 160 + part * PACKED, 16), PACKED)
                total = base[rows, :].astype(jnp.float32) + update[:, part * 256:part * 256 + 256]
                merged[at, k * 160 + part * PACKED:k * 160 + part * PACKED + PACKED] = total.astype(jnp.bfloat16)
        columns = slice(begin * 160, end * 160)
        return jnp.dot(ordered[at, :, columns], merged[at, columns], preferred_element_type=jnp.float32)

    query = project(z1, 0) + project(z1, 1)
    pass_straight(down, late_0)
    from_sibling(down, 1)
    query += project(1 - z1, takes)
    pass_rest(down, (2,))
    from_sibling(down, 2)
    query += project(1 - z1, 1 - takes, (0, 4))
    pass_rest(down, (3,))
    from_sibling(down, 3)
    query += project(1 - z1, 1 - takes, (4, 8))

    gains = gain[...]
    heads = []
    for h in range(2):
        head = query[:, h * 128:h * 128 + 128]
        inverse = lax.rsqrt(jnp.mean(head * head, axis=-1, keepdims=True) + 1e-06)
        heads.append(head * inverse * gains)
    parts = []
    for j in range(4):
        normed = jnp.concatenate([heads[0][j * 8:j * 8 + 8], heads[1][j * 8:j * 8 + 8]], axis=0).astype(jnp.bfloat16)
        values_tile = values[j * 8:j * 8 + 8].reshape(512, 128)
        scores = jnp.dot(normed, turned_keys[j], preferred_element_type=jnp.float32) * (1.0 / math.sqrt(128)) + bias[j]
        expo = jnp.exp(scores - jnp.max(scores, axis=-1, keepdims=True))
        weights = (expo * (1.0 / jnp.sum(expo, axis=-1, keepdims=True))).astype(jnp.bfloat16)
        parts.append(jnp.dot(weights, values_tile, preferred_element_type=jnp.float32))
    out_ref[...] = jnp.concatenate(
        [jnp.concatenate([part[h * 8:h * 8 + 8] for part in parts], axis=0) for h in range(2)], axis=1
    ).astype(jnp.bfloat16)

    def sent(n, sem):
        for kind in (up, down):
            many(kind, n, sem, recv_core.at[0]).wait_send()

    @pl.when(core == 0)
    def _():
        sent(15, send_dp)

    @pl.when(early_0)
    def _():
        sent(15, send_core)

    @pl.when(late_0)
    def _():
        sent(31, send_core)

    @pl.when(early_1)
    def _():
        sent(16, send_dp)
        sent(16, send_core)
        sent(8, send_pair)

    @pl.when(jnp.logical_and(late, crosses))
    def _():
        sent(16, send_dp)


def local(
    hidden, query_base_matrix, input_side_factor, output_side_factor,
    query_norm_gain, cached_key_heads, cached_value_heads, lengths,
):
    bf16 = jnp.bfloat16
    return pl.pallas_call(
        kernel,
        out_shape=jax.ShapeDtypeStruct((32, 256), bf16),
        in_specs=[pl.BlockSpec(memory_space=pltpu.HBM)] * 8,
        out_specs=pl.BlockSpec(memory_space=pltpu.VMEM),
        scratch_shapes=[
            pltpu.VMEM((32, 5120), bf16),
            pltpu.VMEM((5120, 256), bf16),
            pltpu.VMEM((64, 160), bf16),
            pltpu.VMEM((16, 8, 64), bf16),
            pltpu.VMEM((1, 128), jnp.float32),
            pltpu.VMEM((32, 64, 128), bf16),
            pltpu.VMEM((32, 64, 128), bf16),
            pltpu.VMEM((1, 32), jnp.int32),
            pltpu.VMEM((N_DP, PACKED, 128), bf16),
            pltpu.VMEM((N_DP, GROUP, 128), bf16),
            pltpu.VMEM((2, GROUP, 128), bf16),
            pltpu.VMEM((128, 512), bf16),
            pltpu.VMEM((4, 1280, 256), bf16),
            pltpu.VMEM((4, 32, 1280), bf16),
            pltpu.VMEM((4, 128, 512), bf16),
            pltpu.VMEM((4, 16, 512), jnp.float32),
            pltpu.SemaphoreType.DMA((8,)),
            pltpu.SemaphoreType.DMA((2,)),
            pltpu.SemaphoreType.DMA((2,)),
            pltpu.SemaphoreType.DMA((2,)),
            pltpu.SemaphoreType.DMA((N_DP, 2)),
            pltpu.SemaphoreType.DMA((4, 2)),
        ],
        compiler_params=pltpu.CompilerParams(
            collective_id=0, has_side_effects=True, vmem_limit_bytes=54 * 2**20 - 100_000
        ),
        cost_estimate=pl.CostEstimate(flops=260_000_000, bytes_accessed=4_200_000, transcendentals=32768),
    )(
        hidden, query_base_matrix, input_side_factor.T, jnp.transpose(output_side_factor, (1, 2, 0)),
        query_norm_gain.reshape(1, 128), cached_key_heads.reshape(32, 64, 128),
        cached_value_heads.reshape(32, 64, 128), lengths.reshape(1, 32),
    )


def solution(mesh):
    in_specs = (
        P("dp", None),
        P(None, "tensor"),
        P("dp", None),
        P(None, None, "dp"),
        P(),
        P("dp", "tensor", None, None),
        P("dp", "tensor", None, None),
        P("dp"),
    )
    return jax.shard_map(local, mesh=mesh, in_specs=in_specs, out_specs=P("dp", "tensor"), check_vma=False)
```

```python
import functools
import math

import jax
import jax.numpy as jnp
from jax import lax
from jax.experimental import pallas as pl
from jax.experimental.pallas import tpu as pltpu
from jax.sharding import PartitionSpec as P

MESH = pl.DeviceIdType.MESH
N_DP = 32
PACKED = 80
GROUP = 16
SERVE_Y = (0, 1, 2, 3, 7, 6, 5, 4)
AWAIT_Y = (0, 1, 7, 2, 6, 3, 5, 4)


def flip(bit, other):
    return lax.rem(bit + other, 2)


def chunk(half, z):
    return [y * 4 + half * 2 + z for y in AWAIT_Y]


def kernel(
    hidden_hbm, base_hbm, lora_in_hbm, lora_out_hbm, gain_hbm, keys_hbm, values_hbm, lengths_hbm,
    out_ref,
    hidden, base, lora_in, lora_out, gain, keys, values, lengths,
    slots, ups, own_ups, spread, merged, ordered, turned_keys, bias,
    in_sems, send_dp, send_pair, send_core, recv, recv_core,
):
    dp, t = lax.axis_index("dp"), lax.axis_index("tensor")
    x, z_lo, core = t // 4, lax.rem(t // 2, 2), lax.rem(t, 2)
    z1, z0 = lax.rem(dp // 2, 2), lax.rem(dp, 2)
    sibling = (dp, x * 4 + z_lo * 2 + (1 - core))
    early, late = z1 == 0, z1 == 1
    early_0, early_1 = jnp.logical_and(early, core == 0), jnp.logical_and(early, core == 1)
    late_0, late_1 = jnp.logical_and(late, core == 0), jnp.logical_and(late, core == 1)
    takes = 1 - flip(x // 2, lax.rem(x, 2))
    pair = (dp, (x + 1 - 2 * lax.rem(x, 2)) * 4 + z_lo * 2 + core)
    crosses = jnp.logical_and(core == 1, z0 == takes)

    def at(y, z_hi, lo, to_core):
        return (y * 4 + z_hi, x * 4 + lo * 2 + to_core)

    def within(half):
        return [at(y, half * 2 + z, z_lo, 0) for z in range(2) for y in SERVE_Y]

    def across(half, to_core):
        return [at(y, half * 2 + z, flip(z_lo, flip(z0, z + 1)), to_core) for z in range(2) for y in SERVE_Y]

    def crossing_to_here(half, from_core):
        return [at(y, half * 2 + takes, flip(z_lo, flip(z0, takes + 1)), from_core) for y in SERVE_Y]

    def load(i):
        src, dst = (
            (lora_in_hbm, lora_in), (lora_out_hbm, lora_out), (hidden_hbm, hidden), (base_hbm, base),
            (keys_hbm, keys), (values_hbm, values), (gain_hbm, gain), (lengths_hbm, lengths),
        )[i]
        return pltpu.make_async_copy(src, dst, in_sems.at[i])

    for i in (0, 1):
        load(i).start()

    barrier = pltpu.get_barrier_semaphore()

    def signal(device):
        pl.semaphore_signal(barrier, inc=1, device_id=device, device_id_type=MESH)

    @pl.when(late_0)
    def _():
        for device in across(0, 1):
            signal(device)

    @pl.when(core == 0)
    def _():
        for device in within(z1):
            @pl.when(device[0] != dp)
            def _():
                signal(device)

    @pl.when(early_1)
    def _():
        for device in crossing_to_here(1, 1):
            signal(device)
        signal(pair)

    @pl.when(jnp.logical_not(late_0))
    def _():
        signal(sibling)

    @pl.when(early)
    def _():
        for i in range(2, 8):
            load(i).start()

    load(1).wait()
    x_pair = x // 2 * 2
    for lo in range(2):
        columns = []
        for k in range(2):
            even = lora_out[(x_pair + k) * 4 + lo * 2].astype(jnp.float32)
            odd = lora_out[(x_pair + k) * 4 + lo * 2 + 1].astype(jnp.float32)
            columns.append(jnp.concatenate([even, odd], axis=1))
        own_ups[lo] = jnp.concatenate(columns, axis=0).astype(jnp.bfloat16)
    ups[dp] = own_ups[z_lo]

    def prepare():
        for i in range(4, 8):
            load(i).wait()
        square = (32, 128)
        on_diagonal = lax.broadcasted_iota(jnp.int32, square, 0) == lax.broadcasted_iota(jnp.int32, square, 1)
        length_row = jnp.concatenate([lengths[...], jnp.zeros((1, 96), jnp.int32)], axis=1).astype(jnp.float32)
        length_column = jnp.sum(jnp.where(on_diagonal, length_row, 0.0), axis=1, keepdims=True).astype(jnp.int32)
        tile = (16, 512)
        row = lax.rem(lax.broadcasted_iota(jnp.int32, tile, 0), 8)
        column = lax.broadcasted_iota(jnp.int32, tile, 1)
        own_row = column // 64 == row
        position = lax.rem(column, 64)
        for j in range(4):
            length = jnp.concatenate([length_column[j * 8:j * 8 + 8]] * 2, axis=0)
            bias[j] = jnp.where(jnp.logical_and(own_row, position < length), 0.0, -jnp.inf)
            turned_keys[j] = jnp.transpose(keys[j * 8:j * 8 + 8].reshape(512, 128))
        load(2).wait()
        for c in range(4):
            pieces = [hidden[:, s * 160:s * 160 + 160].astype(jnp.float32) for s in chunk(c // 2, c % 2)]
            ordered[c] = jnp.concatenate(pieces, axis=1).astype(jnp.bfloat16)
        load(3).wait()

    @pl.when(early)
    def _():
        prepare()

    @pl.when(jnp.logical_or(jnp.logical_not(late_1), crosses))
    def _():
        pl.semaphore_wait(barrier, jnp.where(early_1, 18, 16))

    def remote(src, dst, send_sem, recv_sem, device):
        return pltpu.make_async_remote_copy(
            src_ref=src, dst_ref=dst, send_sem=send_sem, recv_sem=recv_sem, device_id=device, device_id_type=MESH
        )

    def down(s, send_sem, recv_sem, device):
        return remote(slots.at[s], slots.at[s], send_sem.at[0], recv_sem.at[0], device)

    def up(s, send_sem, recv_sem, device):
        return remote(ups.at[s], ups.at[s], send_sem.at[1], recv_sem.at[1], device)

    def own_up(device):
        z_lo_there = lax.rem(device[1] // 2, 2)
        return remote(own_ups.at[z_lo_there], ups.at[dp], send_dp.at[1], recv.at[dp, 1], device)

    def own_down(device):
        return down(dp, send_dp, recv.at[dp], device)

    def many(kind, n, send_sem, recv_sem):
        ref, at = (slots, 0) if kind is down else (ups, 1)
        return remote(ref.at[pl.ds(0, n)], ref.at[pl.ds(0, n)], send_sem.at[at], recv_sem.at[at], sibling)

    def serve(act):
        @pl.when(jnp.logical_and(late, crosses))
        def _():
            for device in across(0, 1):
                act(device)

        @pl.when(early_1)
        def _():
            for device in across(1, 0):
                act(device)

        @pl.when(core == 0)
        def _():
            for device in within(z1):
                @pl.when(device[0] != dp)
                def _():
                    act(device)

    serve(lambda device: own_up(device).start())

    load(0).wait()
    rows = jnp.transpose(lora_in[...].astype(jnp.float32))
    packed = jnp.concatenate([rows[:PACKED], rows[PACKED:]], axis=1)
    slots[dp] = packed.astype(jnp.bfloat16)

    serve(lambda device: own_down(device).start())

    @pl.when(late)
    def _():
        for i in range(2, 8):
            load(i).start()

    def half_shards(half):
        return chunk(half, 0) + chunk(half, 1)

    def pass_on(kind, s, group):
        kind(s, send_core, recv.at[s], sibling).wait_recv()
        kind(s, send_core, recv_core.at[group], sibling).start()

    def pass_own(kind):
        @pl.when(core == 0)
        def _():
            for s in half_shards(z1):
                @pl.when(s != dp)
                def _():
                    pass_on(kind, s, 0)

    others = chunk(1 - z1, takes) + chunk(1 - z1, 1 - takes)

    def pass_straight(kind, role):
        @pl.when(role)
        def _():
            for s in others[:8]:
                pass_on(kind, s, 1)

                @pl.when(early)
                def _():
                    kind(s, send_pair, recv.at[s], pair).start()

    def pass_rest(kind, groups=(2, 3)):
        @pl.when(jnp.logical_or(late_0, early_1))
        def _():
            for group in groups:
                for s in others[group * 4:group * 4 + 4]:
                    pass_on(kind, s, group)

    def from_sibling(kind, group):
        role = core == 1 if group == 0 else jnp.logical_or(early_0, late_1)

        @pl.when(role)
        def _():
            many(kind, (15, 8, 4, 4)[group], send_core, recv_core.at[group]).wait_recv()

    pass_own(up)
    pass_own(down)

    @pl.when(late)
    def _():
        prepare()

    pass_straight(up, jnp.logical_or(late_0, early_1))
    pass_straight(down, early_1)
    pass_rest(up)
    from_sibling(up, 0)
    from_sibling(down, 0)
    from_sibling(up, 1)
    from_sibling(up, 2)
    from_sibling(up, 3)

    lows = ups[...].astype(jnp.float32)
    both = jnp.where(lax.rem(x, 2) == 0, lows[:, :8], lows[:, 8:]).reshape(256, 128)
    turned = pltpu.roll(both, 64, 1)
    lane = lax.broadcasted_iota(jnp.int32, (128, 256), 0)
    first = jnp.transpose(jnp.where(core == 0, both, turned))
    second = jnp.transpose(jnp.where(core == 0, turned, both))
    spread[:, :256] = jnp.where(lane < 64, first, 0.0).astype(jnp.bfloat16)
    spread[:, 256:] = jnp.where(lane >= 64, second, 0.0).astype(jnp.bfloat16)

    def project(half, z, places=(0, 8)):
        at = half * 2 + z
        begin, end = places
        for k, s in enumerate(chunk(half, z)):
            if not begin <= k < end:
                continue
            update = jnp.dot(slots[s], spread[...], preferred_element_type=jnp.float32)
            for part in range(2):
                rows = pl.ds(pl.multiple_of(s * 160 + part * PACKED, 16), PACKED)
                total = base[rows, :].astype(jnp.float32) + update[:, part * 256:part * 256 + 256]
                merged[at, k * 160 + part * PACKED:k * 160 + part * PACKED + PACKED] = total.astype(jnp.bfloat16)
        columns = slice(begin * 160, end * 160)
        return jnp.dot(ordered[at, :, columns], merged[at, columns], preferred_element_type=jnp.float32)

    query = project(z1, 0) + project(z1, 1)
    pass_straight(down, late_0)
    from_sibling(down, 1)
    query += project(1 - z1, takes)
    pass_rest(down, (2,))
    from_sibling(down, 2)
    query += project(1 - z1, 1 - takes, (0, 4))
    pass_rest(down, (3,))
    from_sibling(down, 3)
    query += project(1 - z1, 1 - takes, (4, 8))

    gains = gain[...]
    heads = []
    for h in range(2):
        head = query[:, h * 128:h * 128 + 128]
        inverse = lax.rsqrt(jnp.mean(head * head, axis=-1, keepdims=True) + 1e-06)
        heads.append(head * inverse * gains)
    parts = []
    for j in range(4):
        normed = jnp.concatenate([heads[0][j * 8:j * 8 + 8], heads[1][j * 8:j * 8 + 8]], axis=0).astype(jnp.bfloat16)
        values_tile = values[j * 8:j * 8 + 8].reshape(512, 128)
        scores = jnp.dot(normed, turned_keys[j], preferred_element_type=jnp.float32) * (1.0 / math.sqrt(128)) + bias[j]
        expo = jnp.exp(scores - jnp.max(scores, axis=-1, keepdims=True))
        weights = (expo * (1.0 / jnp.sum(expo, axis=-1, keepdims=True))).astype(jnp.bfloat16)
        parts.append(jnp.dot(weights, values_tile, preferred_element_type=jnp.float32))
    out_ref[...] = jnp.concatenate(
        [jnp.concatenate([part[h * 8:h * 8 + 8] for part in parts], axis=0) for h in range(2)], axis=1
    ).astype(jnp.bfloat16)

    def sent(n, sem):
        for kind in (up, down):
            many(kind, n, sem, recv_core.at[0]).wait_send()

    @pl.when(core == 0)
    def _():
        sent(15, send_dp)

    @pl.when(early_0)
    def _():
        sent(15, send_core)

    @pl.when(late_0)
    def _():
        sent(31, send_core)

    @pl.when(early_1)
    def _():
        sent(16, send_dp)
        sent(16, send_core)
        sent(8, send_pair)

    @pl.when(jnp.logical_and(late, crosses))
    def _():
        sent(16, send_dp)


def local(
    hidden, query_base_matrix, input_side_factor, output_side_factor,
    query_norm_gain, cached_key_heads, cached_value_heads, lengths,
):
    bf16 = jnp.bfloat16
    return pl.pallas_call(
        kernel,
        out_shape=jax.ShapeDtypeStruct((32, 256), bf16),
        in_specs=[pl.BlockSpec(memory_space=pltpu.HBM)] * 8,
        out_specs=pl.BlockSpec(memory_space=pltpu.VMEM),
        scratch_shapes=[
            pltpu.VMEM((32, 5120), bf16),
            pltpu.VMEM((5120, 256), bf16),
            pltpu.VMEM((64, 160), bf16),
            pltpu.VMEM((16, 8, 64), bf16),
            pltpu.VMEM((1, 128), jnp.float32),
            pltpu.VMEM((32, 64, 128), bf16),
            pltpu.VMEM((32, 64, 128), bf16),
            pltpu.VMEM((1, 32), jnp.int32),
            pltpu.VMEM((N_DP, PACKED, 128), bf16),
            pltpu.VMEM((N_DP, GROUP, 128), bf16),
            pltpu.VMEM((2, GROUP, 128), bf16),
            pltpu.VMEM((128, 512), bf16),
            pltpu.VMEM((4, 1280, 256), bf16),
            pltpu.VMEM((4, 32, 1280), bf16),
            pltpu.VMEM((4, 128, 512), bf16),
            pltpu.VMEM((4, 16, 512), jnp.float32),
            pltpu.SemaphoreType.DMA((8,)),
            pltpu.SemaphoreType.DMA((2,)),
            pltpu.SemaphoreType.DMA((2,)),
            pltpu.SemaphoreType.DMA((2,)),
            pltpu.SemaphoreType.DMA((N_DP, 2)),
            pltpu.SemaphoreType.DMA((4, 2)),
        ],
        compiler_params=pltpu.CompilerParams(
            collective_id=0, has_side_effects=True, vmem_limit_bytes=54 * 2**20 - 100_000
        ),
        cost_estimate=pl.CostEstimate(flops=260_000_000, bytes_accessed=4_200_000, transcendentals=32768),
    )(
        hidden, query_base_matrix, input_side_factor.T, jnp.transpose(output_side_factor, (1, 2, 0)),
        query_norm_gain.reshape(1, 128), cached_key_heads.reshape(32, 64, 128),
        cached_value_heads.reshape(32, 64, 128), lengths.reshape(1, 32),
    )


def solution(mesh):
    in_specs = (
        P("dp", None),
        P(None, "tensor"),
        P("dp", None),
        P(None, None, "dp"),
        P(),
        P("dp", "tensor", None, None),
        P("dp", "tensor", None, None),
        P("dp"),
    )
    return jax.shard_map(local, mesh=mesh, in_specs=in_specs, out_specs=P("dp", "tensor"), check_vma=False)
```

```python
import functools
import math

import jax
import jax.numpy as jnp
from jax import lax
from jax.experimental import pallas as pl
from jax.experimental.pallas import tpu as pltpu
from jax.sharding import PartitionSpec as P

MESH = pl.DeviceIdType.MESH
N_DP = 32
PACKED = 80
GROUP = 16
SERVE_Y = (0, 1, 2, 3, 7, 6, 5, 4)
AWAIT_Y = (0, 1, 7, 2, 6, 3, 5, 4)


def flip(bit, other):
    return lax.rem(bit + other, 2)


def chunk(half, z):
    return [y * 4 + half * 2 + z for y in AWAIT_Y]


def kernel(
    hidden_hbm, base_hbm, lora_in_hbm, lora_out_hbm, gain_hbm, keys_hbm, values_hbm, lengths_hbm,
    out_ref,
    hidden, base, lora_in, lora_out, gain, keys, values, lengths,
    slots, ups, own_ups, spread, merged, ordered, turned_keys, bias,
    in_sems, send_dp, send_pair, send_core, recv, recv_core,
):
    dp, t = lax.axis_index("dp"), lax.axis_index("tensor")
    x, z_lo, core = t // 4, lax.rem(t // 2, 2), lax.rem(t, 2)
    z1, z0 = lax.rem(dp // 2, 2), lax.rem(dp, 2)
    sibling = (dp, x * 4 + z_lo * 2 + (1 - core))
    early, late = z1 == 0, z1 == 1
    early_0, early_1 = jnp.logical_and(early, core == 0), jnp.logical_and(early, core == 1)
    late_0, late_1 = jnp.logical_and(late, core == 0), jnp.logical_and(late, core == 1)
    takes = 1 - flip(x // 2, lax.rem(x, 2))
    pair = (dp, (x + 1 - 2 * lax.rem(x, 2)) * 4 + z_lo * 2 + core)
    crosses = jnp.logical_and(core == 1, z0 == takes)

    def at(y, z_hi, lo, to_core):
        return (y * 4 + z_hi, x * 4 + lo * 2 + to_core)

    def within(half):
        return [at(y, half * 2 + z, z_lo, 0) for z in range(2) for y in SERVE_Y]

    def across(half, to_core):
        return [at(y, half * 2 + z, flip(z_lo, flip(z0, z + 1)), to_core) for z in range(2) for y in SERVE_Y]

    def crossing_to_here(half, from_core):
        return [at(y, half * 2 + takes, flip(z_lo, flip(z0, takes + 1)), from_core) for y in SERVE_Y]

    def load(i):
        src, dst = (
            (lora_in_hbm, lora_in), (lora_out_hbm, lora_out), (hidden_hbm, hidden), (base_hbm, base),
            (keys_hbm, keys), (values_hbm, values), (gain_hbm, gain), (lengths_hbm, lengths),
        )[i]
        return pltpu.make_async_copy(src, dst, in_sems.at[i])

    for i in (0, 1):
        load(i).start()

    barrier = pltpu.get_barrier_semaphore()

    def signal(device):
        pl.semaphore_signal(barrier, inc=1, device_id=device, device_id_type=MESH)

    @pl.when(late_0)
    def _():
        for device in across(0, 1):
            signal(device)

    @pl.when(core == 0)
    def _():
        for device in within(z1):
            @pl.when(device[0] != dp)
            def _():
                signal(device)

    @pl.when(early_1)
    def _():
        for device in crossing_to_here(1, 1):
            signal(device)
        signal(pair)

    @pl.when(jnp.logical_not(late_0))
    def _():
        signal(sibling)

    @pl.when(early)
    def _():
        for i in range(2, 8):
            load(i).start()

    load(1).wait()
    x_pair = x // 2 * 2
    for lo in range(2):
        columns = []
        for k in range(2):
            even = lora_out[(x_pair + k) * 4 + lo * 2].astype(jnp.float32)
            odd = lora_out[(x_pair + k) * 4 + lo * 2 + 1].astype(jnp.float32)
            columns.append(jnp.concatenate([even, odd], axis=1))
        own_ups[lo] = jnp.concatenate(columns, axis=0).astype(jnp.bfloat16)
    ups[dp] = own_ups[z_lo]

    def prepare():
        for i in range(4, 8):
            load(i).wait()
        square = (32, 128)
        on_diagonal = lax.broadcasted_iota(jnp.int32, square, 0) == lax.broadcasted_iota(jnp.int32, square, 1)
        length_row = jnp.concatenate([lengths[...], jnp.zeros((1, 96), jnp.int32)], axis=1).astype(jnp.float32)
        length_column = jnp.sum(jnp.where(on_diagonal, length_row, 0.0), axis=1, keepdims=True).astype(jnp.int32)
        tile = (16, 512)
        row = lax.rem(lax.broadcasted_iota(jnp.int32, tile, 0), 8)
        column = lax.broadcasted_iota(jnp.int32, tile, 1)
        own_row = column // 64 == row
        position = lax.rem(column, 64)
        for j in range(4):
            length = jnp.concatenate([length_column[j * 8:j * 8 + 8]] * 2, axis=0)
            bias[j] = jnp.where(jnp.logical_and(own_row, position < length), 0.0, -jnp.inf)
            turned_keys[j] = jnp.transpose(keys[j * 8:j * 8 + 8].reshape(512, 128))
        load(2).wait()
        for c in range(4):
            pieces = [hidden[:, s * 160:s * 160 + 160].astype(jnp.float32) for s in chunk(c // 2, c % 2)]
            ordered[c] = jnp.concatenate(pieces, axis=1).astype(jnp.bfloat16)
        load(3).wait()

    @pl.when(early)
    def _():
        prepare()

    @pl.when(jnp.logical_or(jnp.logical_not(late_1), crosses))
    def _():
        pl.semaphore_wait(barrier, jnp.where(early_1, 18, 16))

    def remote(src, dst, send_sem, recv_sem, device):
        return pltpu.make_async_remote_copy(
            src_ref=src, dst_ref=dst, send_sem=send_sem, recv_sem=recv_sem, device_id=device, device_id_type=MESH
        )

    def down(s, send_sem, recv_sem, device):
        return remote(slots.at[s], slots.at[s], send_sem.at[0], recv_sem.at[0], device)

    def up(s, send_sem, recv_sem, device):
        return remote(ups.at[s], ups.at[s], send_sem.at[1], recv_sem.at[1], device)

    def own_up(device):
        z_lo_there = lax.rem(device[1] // 2, 2)
        return remote(own_ups.at[z_lo_there], ups.at[dp], send_dp.at[1], recv.at[dp, 1], device)

    def own_down(device):
        return down(dp, send_dp, recv.at[dp], device)

    def many(kind, n, send_sem, recv_sem):
        ref, at = (slots, 0) if kind is down else (ups, 1)
        return remote(ref.at[pl.ds(0, n)], ref.at[pl.ds(0, n)], send_sem.at[at], recv_sem.at[at], sibling)

    def serve(act):
        @pl.when(jnp.logical_and(late, crosses))
        def _():
            for device in across(0, 1):
                act(device)

        @pl.when(early_1)
        def _():
            for device in across(1, 0):
                act(device)

        @pl.when(core == 0)
        def _():
            for device in within(z1):
                @pl.when(device[0] != dp)
                def _():
                    act(device)

    serve(lambda device: own_up(device).start())

    load(0).wait()
    rows = jnp.transpose(lora_in[...].astype(jnp.float32))
    packed = jnp.concatenate([rows[:PACKED], rows[PACKED:]], axis=1)
    slots[dp] = packed.astype(jnp.bfloat16)

    serve(lambda device: own_down(device).start())

    @pl.when(late)
    def _():
        for i in range(2, 8):
            load(i).start()

    def half_shards(half):
        return chunk(half, 0) + chunk(half, 1)

    def pass_on(kind, s, group):
        kind(s, send_core, recv.at[s], sibling).wait_recv()
        kind(s, send_core, recv_core.at[group], sibling).start()

    def pass_own(kind):
        @pl.when(core == 0)
        def _():
            for s in half_shards(z1):
                @pl.when(s != dp)
                def _():
                    pass_on(kind, s, 0)

    others = chunk(1 - z1, takes) + chunk(1 - z1, 1 - takes)

    def pass_straight(kind, role):
        @pl.when(role)
        def _():
            for s in others[:8]:
                pass_on(kind, s, 1)

                @pl.when(early)
                def _():
                    kind(s, send_pair, recv.at[s], pair).start()

    def pass_rest(kind, groups=(2, 3)):
        @pl.when(jnp.logical_or(late_0, early_1))
        def _():
            for group in groups:
                for k, s in enumerate(others[group * 4:group * 4 + 4]):
                    pass_on(kind, s, 4 if group == 3 and k > 1 else group)

    def from_sibling(kind, group):
        role = core == 1 if group == 0 else jnp.logical_or(early_0, late_1)

        @pl.when(role)
        def _():
            many(kind, (15, 8, 4, 2, 2)[group], send_core, recv_core.at[group]).wait_recv()

    pass_own(up)
    pass_own(down)

    @pl.when(late)
    def _():
        prepare()

    pass_straight(up, jnp.logical_or(late_0, early_1))
    pass_straight(down, early_1)
    pass_rest(up)
    from_sibling(up, 0)
    from_sibling(down, 0)
    from_sibling(up, 1)
    from_sibling(up, 2)
    from_sibling(up, 3)
    from_sibling(up, 4)

    lows = ups[...].astype(jnp.float32)
    both = jnp.where(lax.rem(x, 2) == 0, lows[:, :8], lows[:, 8:]).reshape(256, 128)
    turned = pltpu.roll(both, 64, 1)
    lane = lax.broadcasted_iota(jnp.int32, (128, 256), 0)
    first = jnp.transpose(jnp.where(core == 0, both, turned))
    second = jnp.transpose(jnp.where(core == 0, turned, both))
    spread[:, :256] = jnp.where(lane < 64, first, 0.0).astype(jnp.bfloat16)
    spread[:, 256:] = jnp.where(lane >= 64, second, 0.0).astype(jnp.bfloat16)

    def project(half, z, places=(0, 8)):
        at = half * 2 + z
        begin, end = places
        for k, s in enumerate(chunk(half, z)):
            if not begin <= k < end:
                continue
            update = jnp.dot(slots[s], spread[...], preferred_element_type=jnp.float32)
            for part in range(2):
                rows = pl.ds(pl.multiple_of(s * 160 + part * PACKED, 16), PACKED)
                total = base[rows, :].astype(jnp.float32) + update[:, part * 256:part * 256 + 256]
                merged[at, k * 160 + part * PACKED:k * 160 + part * PACKED + PACKED] = total.astype(jnp.bfloat16)
        columns = slice(begin * 160, end * 160)
        return jnp.dot(ordered[at, :, columns], merged[at, columns], preferred_element_type=jnp.float32)

    query = project(z1, 0) + project(z1, 1)
    pass_straight(down, late_0)
    from_sibling(down, 1)
    query += project(1 - z1, takes)
    pass_rest(down, (2,))
    from_sibling(down, 2)
    query += project(1 - z1, 1 - takes, (0, 4))
    pass_rest(down, (3,))
    from_sibling(down, 3)
    query += project(1 - z1, 1 - takes, (4, 6))
    from_sibling(down, 4)
    query += project(1 - z1, 1 - takes, (6, 8))

    gains = gain[...]
    heads = []
    for h in range(2):
        head = query[:, h * 128:h * 128 + 128]
        inverse = lax.rsqrt(jnp.mean(head * head, axis=-1, keepdims=True) + 1e-06)
        heads.append(head * inverse * gains)
    parts = []
    for j in range(4):
        normed = jnp.concatenate([heads[0][j * 8:j * 8 + 8], heads[1][j * 8:j * 8 + 8]], axis=0).astype(jnp.bfloat16)
        values_tile = values[j * 8:j * 8 + 8].reshape(512, 128)
        scores = jnp.dot(normed, turned_keys[j], preferred_element_type=jnp.float32) * (1.0 / math.sqrt(128)) + bias[j]
        expo = jnp.exp(scores - jnp.max(scores, axis=-1, keepdims=True))
        weights = (expo * (1.0 / jnp.sum(expo, axis=-1, keepdims=True))).astype(jnp.bfloat16)
        parts.append(jnp.dot(weights, values_tile, preferred_element_type=jnp.float32))
    out_ref[...] = jnp.concatenate(
        [jnp.concatenate([part[h * 8:h * 8 + 8] for part in parts], axis=0) for h in range(2)], axis=1
    ).astype(jnp.bfloat16)

    def sent(n, sem):
        for kind in (up, down):
            many(kind, n, sem, recv_core.at[0]).wait_send()

    @pl.when(core == 0)
    def _():
        sent(15, send_dp)

    @pl.when(early_0)
    def _():
        sent(15, send_core)

    @pl.when(late_0)
    def _():
        sent(31, send_core)

    @pl.when(early_1)
    def _():
        sent(16, send_dp)
        sent(16, send_core)
        sent(8, send_pair)

    @pl.when(jnp.logical_and(late, crosses))
    def _():
        sent(16, send_dp)


def local(
    hidden, query_base_matrix, input_side_factor, output_side_factor,
    query_norm_gain, cached_key_heads, cached_value_heads, lengths,
):
    bf16 = jnp.bfloat16
    return pl.pallas_call(
        kernel,
        out_shape=jax.ShapeDtypeStruct((32, 256), bf16),
        in_specs=[pl.BlockSpec(memory_space=pltpu.HBM)] * 8,
        out_specs=pl.BlockSpec(memory_space=pltpu.VMEM),
        scratch_shapes=[
            pltpu.VMEM((32, 5120), bf16),
            pltpu.VMEM((5120, 256), bf16),
            pltpu.VMEM((64, 160), bf16),
            pltpu.VMEM((16, 8, 64), bf16),
            pltpu.VMEM((1, 128), jnp.float32),
            pltpu.VMEM((32, 64, 128), bf16),
            pltpu.VMEM((32, 64, 128), bf16),
            pltpu.VMEM((1, 32), jnp.int32),
            pltpu.VMEM((N_DP, PACKED, 128), bf16),
            pltpu.VMEM((N_DP, GROUP, 128), bf16),
            pltpu.VMEM((2, GROUP, 128), bf16),
            pltpu.VMEM((128, 512), bf16),
            pltpu.VMEM((4, 1280, 256), bf16),
            pltpu.VMEM((4, 32, 1280), bf16),
            pltpu.VMEM((4, 128, 512), bf16),
            pltpu.VMEM((4, 16, 512), jnp.float32),
            pltpu.SemaphoreType.DMA((8,)),
            pltpu.SemaphoreType.DMA((2,)),
            pltpu.SemaphoreType.DMA((2,)),
            pltpu.SemaphoreType.DMA((2,)),
            pltpu.SemaphoreType.DMA((N_DP, 2)),
            pltpu.SemaphoreType.DMA((5, 2)),
        ],
        compiler_params=pltpu.CompilerParams(
            collective_id=0, has_side_effects=True, vmem_limit_bytes=54 * 2**20 - 100_000
        ),
        cost_estimate=pl.CostEstimate(flops=260_000_000, bytes_accessed=4_200_000, transcendentals=32768),
    )(
        hidden, query_base_matrix, input_side_factor.T, jnp.transpose(output_side_factor, (1, 2, 0)),
        query_norm_gain.reshape(1, 128), cached_key_heads.reshape(32, 64, 128),
        cached_value_heads.reshape(32, 64, 128), lengths.reshape(1, 32),
    )


def solution(mesh):
    in_specs = (
        P("dp", None),
        P(None, "tensor"),
        P("dp", None),
        P(None, None, "dp"),
        P(),
        P("dp", "tensor", None, None),
        P("dp", "tensor", None, None),
        P("dp"),
    )
    return jax.shard_map(local, mesh=mesh, in_specs=in_specs, out_specs=P("dp", "tensor"), check_vma=False)
```

```python
import functools
import math

import jax
import jax.numpy as jnp
from jax import lax
from jax.experimental import pallas as pl
from jax.experimental.pallas import tpu as pltpu
from jax.sharding import PartitionSpec as P

MESH = pl.DeviceIdType.MESH
N_DP = 32
PACKED = 80
GROUP = 16
SERVE_Y = (0, 1, 2, 3, 7, 6, 5, 4)
AWAIT_Y = (0, 1, 7, 2, 6, 3, 5, 4)


def flip(bit, other):
    return lax.rem(bit + other, 2)


def chunk(half, z):
    return [y * 4 + half * 2 + z for y in AWAIT_Y]


def kernel(
    hidden_hbm, base_hbm, lora_in_hbm, lora_out_hbm, gain_hbm, keys_hbm, values_hbm, lengths_hbm,
    out_ref,
    hidden, base, lora_in, lora_out, gain, keys, values, lengths,
    slots, ups, own_ups, spread, merged, ordered, turned_keys, bias,
    in_sems, send_dp, send_pair, send_core, recv, recv_core,
):
    dp, t = lax.axis_index("dp"), lax.axis_index("tensor")
    x, z_lo, core = t // 4, lax.rem(t // 2, 2), lax.rem(t, 2)
    z1, z0 = lax.rem(dp // 2, 2), lax.rem(dp, 2)
    sibling = (dp, x * 4 + z_lo * 2 + (1 - core))
    early, late = z1 == 0, z1 == 1
    early_0, early_1 = jnp.logical_and(early, core == 0), jnp.logical_and(early, core == 1)
    late_0, late_1 = jnp.logical_and(late, core == 0), jnp.logical_and(late, core == 1)
    takes = 1 - flip(x // 2, lax.rem(x, 2))
    pair = (dp, (x + 1 - 2 * lax.rem(x, 2)) * 4 + z_lo * 2 + core)
    crosses = jnp.logical_and(core == 1, z0 == takes)

    def at(y, z_hi, lo, to_core):
        return (y * 4 + z_hi, x * 4 + lo * 2 + to_core)

    def within(half):
        return [at(y, half * 2 + z, z_lo, 0) for z in range(2) for y in SERVE_Y]

    def across(half, to_core):
        return [at(y, half * 2 + z, flip(z_lo, flip(z0, z + 1)), to_core) for z in range(2) for y in SERVE_Y]

    def crossing_to_here(half, from_core):
        return [at(y, half * 2 + takes, flip(z_lo, flip(z0, takes + 1)), from_core) for y in SERVE_Y]

    def load(i):
        src, dst = (
            (lora_in_hbm, lora_in), (lora_out_hbm, lora_out), (hidden_hbm, hidden), (base_hbm, base),
            (keys_hbm, keys), (values_hbm, values), (gain_hbm, gain), (lengths_hbm, lengths),
        )[i]
        return pltpu.make_async_copy(src, dst, in_sems.at[i])

    for i in (0, 1):
        load(i).start()

    barrier = pltpu.get_barrier_semaphore()

    def signal(device):
        pl.semaphore_signal(barrier, inc=1, device_id=device, device_id_type=MESH)

    @pl.when(late_0)
    def _():
        for device in across(0, 1):
            signal(device)

    @pl.when(core == 0)
    def _():
        for device in within(z1):
            @pl.when(device[0] != dp)
            def _():
                signal(device)

    @pl.when(early_1)
    def _():
        for device in crossing_to_here(1, 1):
            signal(device)
        signal(pair)

    @pl.when(jnp.logical_not(late_0))
    def _():
        signal(sibling)

    @pl.when(early)
    def _():
        for i in range(2, 8):
            load(i).start()

    load(1).wait()
    x_pair = x // 2 * 2
    for lo in range(2):
        columns = []
        for k in range(2):
            even = lora_out[(x_pair + k) * 4 + lo * 2].astype(jnp.float32)
            odd = lora_out[(x_pair + k) * 4 + lo * 2 + 1].astype(jnp.float32)
            columns.append(jnp.concatenate([even, odd], axis=1))
        own_ups[lo] = jnp.concatenate(columns, axis=0).astype(jnp.bfloat16)
    ups[dp] = own_ups[z_lo]

    def prepare():
        for i in range(4, 8):
            load(i).wait()
        square = (32, 128)
        on_diagonal = lax.broadcasted_iota(jnp.int32, square, 0) == lax.broadcasted_iota(jnp.int32, square, 1)
        length_row = jnp.concatenate([lengths[...], jnp.zeros((1, 96), jnp.int32)], axis=1).astype(jnp.float32)
        length_column = jnp.sum(jnp.where(on_diagonal, length_row, 0.0), axis=1, keepdims=True).astype(jnp.int32)
        tile = (16, 512)
        row = lax.rem(lax.broadcasted_iota(jnp.int32, tile, 0), 8)
        column = lax.broadcasted_iota(jnp.int32, tile, 1)
        own_row = column // 64 == row
        position = lax.rem(column, 64)
        for j in range(4):
            length = jnp.concatenate([length_column[j * 8:j * 8 + 8]] * 2, axis=0)
            bias[j] = jnp.where(jnp.logical_and(own_row, position < length), 0.0, -jnp.inf)
            turned_keys[j] = jnp.transpose(keys[j * 8:j * 8 + 8].reshape(512, 128))
        load(2).wait()
        for c in range(4):
            pieces = [hidden[:, s * 160:s * 160 + 160].astype(jnp.float32) for s in chunk(c // 2, c % 2)]
            ordered[c] = jnp.concatenate(pieces, axis=1).astype(jnp.bfloat16)
        load(3).wait()

    @pl.when(early)
    def _():
        prepare()

    @pl.when(jnp.logical_or(jnp.logical_not(late_1), crosses))
    def _():
        pl.semaphore_wait(barrier, jnp.where(early_1, 18, 16))

    def remote(src, dst, send_sem, recv_sem, device):
        return pltpu.make_async_remote_copy(
            src_ref=src, dst_ref=dst, send_sem=send_sem, recv_sem=recv_sem, device_id=device, device_id_type=MESH
        )

    def down(s, send_sem, recv_sem, device):
        return remote(slots.at[s], slots.at[s], send_sem.at[0], recv_sem.at[0], device)

    def up(s, send_sem, recv_sem, device):
        return remote(ups.at[s], ups.at[s], send_sem.at[1], recv_sem.at[1], device)

    def own_up(device):
        z_lo_there = lax.rem(device[1] // 2, 2)
        return remote(own_ups.at[z_lo_there], ups.at[dp], send_dp.at[1], recv.at[dp, 1], device)

    def own_down(device):
        return down(dp, send_dp, recv.at[dp], device)

    def many(kind, n, send_sem, recv_sem):
        ref, at = (slots, 0) if kind is down else (ups, 1)
        return remote(ref.at[pl.ds(0, n)], ref.at[pl.ds(0, n)], send_sem.at[at], recv_sem.at[at], sibling)

    def serve(act):
        @pl.when(jnp.logical_and(late, crosses))
        def _():
            for device in across(0, 1):
                act(device)

        @pl.when(early_1)
        def _():
            for device in across(1, 0):
                act(device)

        @pl.when(early_0)
        def _():
            serve_within(act)

    def serve_within(act):
        for device in within(z1):
            @pl.when(device[0] != dp)
            def _():
                act(device)

    serve(lambda device: own_up(device).start())

    @pl.when(late_0)
    def _():
        serve_within(lambda device: own_up(device).start())

    load(0).wait()
    rows = jnp.transpose(lora_in[...].astype(jnp.float32))
    packed = jnp.concatenate([rows[:PACKED], rows[PACKED:]], axis=1)
    slots[dp] = packed.astype(jnp.bfloat16)

    serve(lambda device: own_down(device).start())

    @pl.when(late)
    def _():
        for i in range(2, 8):
            load(i).start()

    def half_shards(half):
        return chunk(half, 0) + chunk(half, 1)

    def pass_on(kind, s, group):
        kind(s, send_core, recv.at[s], sibling).wait_recv()
        kind(s, send_core, recv_core.at[group], sibling).start()

    def pass_own(kind):
        @pl.when(core == 0)
        def _():
            for s in half_shards(z1):
                @pl.when(s != dp)
                def _():
                    pass_on(kind, s, 0)

    others = chunk(1 - z1, takes) + chunk(1 - z1, 1 - takes)

    def pass_straight(kind, role):
        @pl.when(role)
        def _():
            for s in others[:8]:
                pass_on(kind, s, 1)

                @pl.when(early)
                def _():
                    kind(s, send_pair, recv.at[s], pair).start()

    def pass_rest(kind, groups=(2, 3)):
        @pl.when(jnp.logical_or(late_0, early_1))
        def _():
            for group in groups:
                for s in others[group * 4:group * 4 + 4]:
                    pass_on(kind, s, group)

    def from_sibling(kind, group):
        role = core == 1 if group == 0 else jnp.logical_or(early_0, late_1)

        @pl.when(role)
        def _():
            many(kind, (15, 8, 4, 4)[group], send_core, recv_core.at[group]).wait_recv()

    pass_own(up)

    @pl.when(late_0)
    def _():
        serve_within(lambda device: own_down(device).start())

    pass_own(down)

    @pl.when(late)
    def _():
        prepare()

    pass_straight(up, jnp.logical_or(late_0, early_1))
    pass_straight(down, early_1)
    pass_rest(up)
    from_sibling(up, 0)
    from_sibling(down, 0)
    from_sibling(up, 1)
    from_sibling(up, 2)
    from_sibling(up, 3)

    lows = ups[...].astype(jnp.float32)
    both = jnp.where(lax.rem(x, 2) == 0, lows[:, :8], lows[:, 8:]).reshape(256, 128)
    turned = pltpu.roll(both, 64, 1)
    lane = lax.broadcasted_iota(jnp.int32, (128, 256), 0)
    first = jnp.transpose(jnp.where(core == 0, both, turned))
    second = jnp.transpose(jnp.where(core == 0, turned, both))
    spread[:, :256] = jnp.where(lane < 64, first, 0.0).astype(jnp.bfloat16)
    spread[:, 256:] = jnp.where(lane >= 64, second, 0.0).astype(jnp.bfloat16)

    def project(half, z, places=(0, 8)):
        at = half * 2 + z
        begin, end = places
        for k, s in enumerate(chunk(half, z)):
            if not begin <= k < end:
                continue
            update = jnp.dot(slots[s], spread[...], preferred_element_type=jnp.float32)
            for part in range(2):
                rows = pl.ds(pl.multiple_of(s * 160 + part * PACKED, 16), PACKED)
                total = base[rows, :].astype(jnp.float32) + update[:, part * 256:part * 256 + 256]
                merged[at, k * 160 + part * PACKED:k * 160 + part * PACKED + PACKED] = total.astype(jnp.bfloat16)
        columns = slice(begin * 160, end * 160)
        return jnp.dot(ordered[at, :, columns], merged[at, columns], preferred_element_type=jnp.float32)

    query = project(z1, 0) + project(z1, 1)
    pass_straight(down, late_0)
    from_sibling(down, 1)
    query += project(1 - z1, takes)
    pass_rest(down, (2,))
    from_sibling(down, 2)
    query += project(1 - z1, 1 - takes, (0, 4))
    pass_rest(down, (3,))
    from_sibling(down, 3)
    query += project(1 - z1, 1 - takes, (4, 8))

    gains = gain[...]
    heads = []
    for h in range(2):
        head = query[:, h * 128:h * 128 + 128]
        inverse = lax.rsqrt(jnp.mean(head * head, axis=-1, keepdims=True) + 1e-06)
        heads.append(head * inverse * gains)
    parts = []
    for j in range(4):
        normed = jnp.concatenate([heads[0][j * 8:j * 8 + 8], heads[1][j * 8:j * 8 + 8]], axis=0).astype(jnp.bfloat16)
        values_tile = values[j * 8:j * 8 + 8].reshape(512, 128)
        scores = jnp.dot(normed, turned_keys[j], preferred_element_type=jnp.float32) * (1.0 / math.sqrt(128)) + bias[j]
        expo = jnp.exp(scores - jnp.max(scores, axis=-1, keepdims=True))
        weights = (expo * (1.0 / jnp.sum(expo, axis=-1, keepdims=True))).astype(jnp.bfloat16)
        parts.append(jnp.dot(weights, values_tile, preferred_element_type=jnp.float32))
    out_ref[...] = jnp.concatenate(
        [jnp.concatenate([part[h * 8:h * 8 + 8] for part in parts], axis=0) for h in range(2)], axis=1
    ).astype(jnp.bfloat16)

    def sent(n, sem):
        for kind in (up, down):
            many(kind, n, sem, recv_core.at[0]).wait_send()

    @pl.when(core == 0)
    def _():
        sent(15, send_dp)

    @pl.when(early_0)
    def _():
        sent(15, send_core)

    @pl.when(late_0)
    def _():
        sent(31, send_core)

    @pl.when(early_1)
    def _():
        sent(16, send_dp)
        sent(16, send_core)
        sent(8, send_pair)

    @pl.when(jnp.logical_and(late, crosses))
    def _():
        sent(16, send_dp)


def local(
    hidden, query_base_matrix, input_side_factor, output_side_factor,
    query_norm_gain, cached_key_heads, cached_value_heads, lengths,
):
    bf16 = jnp.bfloat16
    return pl.pallas_call(
        kernel,
        out_shape=jax.ShapeDtypeStruct((32, 256), bf16),
        in_specs=[pl.BlockSpec(memory_space=pltpu.HBM)] * 8,
        out_specs=pl.BlockSpec(memory_space=pltpu.VMEM),
        scratch_shapes=[
            pltpu.VMEM((32, 5120), bf16),
            pltpu.VMEM((5120, 256), bf16),
            pltpu.VMEM((64, 160), bf16),
            pltpu.VMEM((16, 8, 64), bf16),
            pltpu.VMEM((1, 128), jnp.float32),
            pltpu.VMEM((32, 64, 128), bf16),
            pltpu.VMEM((32, 64, 128), bf16),
            pltpu.VMEM((1, 32), jnp.int32),
            pltpu.VMEM((N_DP, PACKED, 128), bf16),
            pltpu.VMEM((N_DP, GROUP, 128), bf16),
            pltpu.VMEM((2, GROUP, 128), bf16),
            pltpu.VMEM((128, 512), bf16),
            pltpu.VMEM((4, 1280, 256), bf16),
            pltpu.VMEM((4, 32, 1280), bf16),
            pltpu.VMEM((4, 128, 512), bf16),
            pltpu.VMEM((4, 16, 512), jnp.float32),
            pltpu.SemaphoreType.DMA((8,)),
            pltpu.SemaphoreType.DMA((2,)),
            pltpu.SemaphoreType.DMA((2,)),
            pltpu.SemaphoreType.DMA((2,)),
            pltpu.SemaphoreType.DMA((N_DP, 2)),
            pltpu.SemaphoreType.DMA((4, 2)),
        ],
        compiler_params=pltpu.CompilerParams(
            collective_id=0, has_side_effects=True, vmem_limit_bytes=54 * 2**20 - 100_000
        ),
        cost_estimate=pl.CostEstimate(flops=260_000_000, bytes_accessed=4_200_000, transcendentals=32768),
    )(
        hidden, query_base_matrix, input_side_factor.T, jnp.transpose(output_side_factor, (1, 2, 0)),
        query_norm_gain.reshape(1, 128), cached_key_heads.reshape(32, 64, 128),
        cached_value_heads.reshape(32, 64, 128), lengths.reshape(1, 32),
    )


def solution(mesh):
    in_specs = (
        P("dp", None),
        P(None, "tensor"),
        P("dp", None),
        P(None, None, "dp"),
        P(),
        P("dp", "tensor", None, None),
        P("dp", "tensor", None, None),
        P("dp"),
    )
    return jax.shard_map(local, mesh=mesh, in_specs=in_specs, out_specs=P("dp", "tensor"), check_vma=False)
```

```python
import functools
import math

import jax
import jax.numpy as jnp
from jax import lax
from jax.experimental import pallas as pl
from jax.experimental.pallas import tpu as pltpu
from jax.sharding import PartitionSpec as P

MESH = pl.DeviceIdType.MESH
N_DP = 32
PACKED = 80
GROUP = 16
SERVE_Y = (0, 1, 2, 3, 7, 6, 5, 4)
AWAIT_Y = (0, 1, 7, 2, 6, 3, 5, 4)


def flip(bit, other):
    return lax.rem(bit + other, 2)


def chunk(half, z):
    return [y * 4 + half * 2 + z for y in AWAIT_Y]


def kernel(
    hidden_hbm, base_hbm, lora_in_hbm, lora_out_hbm, gain_hbm, keys_hbm, values_hbm, lengths_hbm,
    out_ref,
    hidden, base, lora_in, lora_out, gain, keys, values, lengths,
    slots, ups, own_ups, spread, merged, ordered, turned_keys, bias,
    in_sems, send_dp, send_pair, send_core, recv, recv_core,
):
    dp, t = lax.axis_index("dp"), lax.axis_index("tensor")
    x, z_lo, core = t // 4, lax.rem(t // 2, 2), lax.rem(t, 2)
    z1, z0 = lax.rem(dp // 2, 2), lax.rem(dp, 2)
    sibling = (dp, x * 4 + z_lo * 2 + (1 - core))
    early, late = z1 == 0, z1 == 1
    early_0, early_1 = jnp.logical_and(early, core == 0), jnp.logical_and(early, core == 1)
    late_0, late_1 = jnp.logical_and(late, core == 0), jnp.logical_and(late, core == 1)
    takes = 1 - flip(x // 2, lax.rem(x, 2))
    pair = (dp, (x + 1 - 2 * lax.rem(x, 2)) * 4 + z_lo * 2 + core)
    crosses = jnp.logical_and(core == 1, z0 == takes)

    def at(y, z_hi, lo, to_core):
        return (y * 4 + z_hi, x * 4 + lo * 2 + to_core)

    def within(half):
        return [at(y, half * 2 + z, z_lo, 0) for z in range(2) for y in SERVE_Y]

    def across(half, to_core):
        return [at(y, half * 2 + z, flip(z_lo, flip(z0, z + 1)), to_core) for z in range(2) for y in SERVE_Y]

    def crossing_to_here(half, from_core):
        return [at(y, half * 2 + takes, flip(z_lo, flip(z0, takes + 1)), from_core) for y in SERVE_Y]

    def load(i):
        src, dst = (
            (lora_in_hbm, lora_in), (lora_out_hbm, lora_out), (hidden_hbm, hidden), (base_hbm, base),
            (keys_hbm, keys), (values_hbm, values), (gain_hbm, gain), (lengths_hbm, lengths),
        )[i]
        return pltpu.make_async_copy(src, dst, in_sems.at[i])

    for i in (0, 1):
        load(i).start()

    barrier = pltpu.get_barrier_semaphore()

    def signal(device):
        pl.semaphore_signal(barrier, inc=1, device_id=device, device_id_type=MESH)

    @pl.when(late_0)
    def _():
        for device in across(0, 1):
            signal(device)

    @pl.when(core == 0)
    def _():
        for device in within(z1):
            @pl.when(device[0] != dp)
            def _():
                signal(device)

    @pl.when(early_1)
    def _():
        for device in crossing_to_here(1, 1):
            signal(device)
        signal(pair)

    @pl.when(jnp.logical_not(late_0))
    def _():
        signal(sibling)

    @pl.when(early)
    def _():
        for i in range(2, 8):
            load(i).start()

    load(1).wait()
    x_pair = x // 2 * 2
    for lo in range(2):
        columns = []
        for k in range(2):
            even = lora_out[(x_pair + k) * 4 + lo * 2].astype(jnp.float32)
            odd = lora_out[(x_pair + k) * 4 + lo * 2 + 1].astype(jnp.float32)
            columns.append(jnp.concatenate([even, odd], axis=1))
        own_ups[lo] = jnp.concatenate(columns, axis=0).astype(jnp.bfloat16)
    ups[dp] = own_ups[z_lo]

    def prepare():
        for i in range(4, 8):
            load(i).wait()
        square = (32, 128)
        on_diagonal = lax.broadcasted_iota(jnp.int32, square, 0) == lax.broadcasted_iota(jnp.int32, square, 1)
        length_row = jnp.concatenate([lengths[...], jnp.zeros((1, 96), jnp.int32)], axis=1).astype(jnp.float32)
        length_column = jnp.sum(jnp.where(on_diagonal, length_row, 0.0), axis=1, keepdims=True).astype(jnp.int32)
        tile = (16, 512)
        row = lax.rem(lax.broadcasted_iota(jnp.int32, tile, 0), 8)
        column = lax.broadcasted_iota(jnp.int32, tile, 1)
        own_row = column // 64 == row
        position = lax.rem(column, 64)
        for j in range(4):
            length = jnp.concatenate([length_column[j * 8:j * 8 + 8]] * 2, axis=0)
            bias[j] = jnp.where(jnp.logical_and(own_row, position < length), 0.0, -jnp.inf)
            turned_keys[j] = jnp.transpose(keys[j * 8:j * 8 + 8].reshape(512, 128))
        load(2).wait()
        for c in range(4):
            pieces = [hidden[:, s * 160:s * 160 + 160].astype(jnp.float32) for s in chunk(c // 2, c % 2)]
            ordered[c] = jnp.concatenate(pieces, axis=1).astype(jnp.bfloat16)
        load(3).wait()

    @pl.when(early)
    def _():
        prepare()

    @pl.when(jnp.logical_or(jnp.logical_not(late_1), crosses))
    def _():
        pl.semaphore_wait(barrier, jnp.where(early_1, 18, 16))

    def remote(src, dst, send_sem, recv_sem, device):
        return pltpu.make_async_remote_copy(
            src_ref=src, dst_ref=dst, send_sem=send_sem, recv_sem=recv_sem, device_id=device, device_id_type=MESH
        )

    def down(s, send_sem, recv_sem, device):
        return remote(slots.at[s], slots.at[s], send_sem.at[0], recv_sem.at[0], device)

    def up(s, send_sem, recv_sem, device):
        return remote(ups.at[s], ups.at[s], send_sem.at[1], recv_sem.at[1], device)

    def own_up(device):
        z_lo_there = lax.rem(device[1] // 2, 2)
        return remote(own_ups.at[z_lo_there], ups.at[dp], send_dp.at[1], recv.at[dp, 1], device)

    def own_down(device):
        return down(dp, send_dp, recv.at[dp], device)

    def many(kind, n, send_sem, recv_sem):
        ref, at = (slots, 0) if kind is down else (ups, 1)
        return remote(ref.at[pl.ds(0, n)], ref.at[pl.ds(0, n)], send_sem.at[at], recv_sem.at[at], sibling)

    def serve(act):
        @pl.when(jnp.logical_and(late, crosses))
        def _():
            for device in across(0, 1):
                act(device)

        @pl.when(early_1)
        def _():
            for device in across(1, 0):
                act(device)

        @pl.when(core == 0)
        def _():
            for device in within(z1):
                @pl.when(device[0] != dp)
                def _():
                    act(device)

    serve(lambda device: own_up(device).start())

    load(0).wait()
    rows = jnp.transpose(lora_in[...].astype(jnp.float32))
    packed = jnp.concatenate([rows[:PACKED], rows[PACKED:]], axis=1)
    slots[dp] = packed.astype(jnp.bfloat16)

    serve(lambda device: own_down(device).start())

    @pl.when(late)
    def _():
        for i in range(2, 8):
            load(i).start()

    def half_shards(half):
        return chunk(half, 0) + chunk(half, 1)

    def pass_on(kind, s, group):
        kind(s, send_core, recv.at[s], sibling).wait_recv()
        kind(s, send_core, recv_core.at[group], sibling).start()

    def pass_own(kind):
        @pl.when(core == 0)
        def _():
            for s in half_shards(z1):
                @pl.when(s != dp)
                def _():
                    pass_on(kind, s, 0)

    others = chunk(1 - z1, takes) + chunk(1 - z1, 1 - takes)

    def pass_straight(kind, role):
        @pl.when(role)
        def _():
            for s in others[:8]:
                pass_on(kind, s, 1)

                @pl.when(early)
                def _():
                    kind(s, send_pair, recv.at[s], pair).start()

    def pass_rest(kind, groups=(2, 3)):
        @pl.when(jnp.logical_or(late_0, early_1))
        def _():
            for group in groups:
                for s in others[group * 4:group * 4 + 4]:
                    pass_on(kind, s, group)

    def from_sibling(kind, group):
        role = core == 1 if group == 0 else jnp.logical_or(early_0, late_1)

        @pl.when(role)
        def _():
            many(kind, (15, 8, 4, 4)[group], send_core, recv_core.at[group]).wait_recv()

    pass_own(up)
    pass_own(down)

    @pl.when(late)
    def _():
        prepare()

    pass_straight(up, jnp.logical_or(late_0, early_1))
    pass_straight(down, early_1)
    pass_rest(up)
    from_sibling(up, 0)
    from_sibling(down, 0)
    from_sibling(up, 1)
    from_sibling(up, 2)
    from_sibling(up, 3)

    lows = ups[...].astype(jnp.float32)
    both = jnp.where(lax.rem(x, 2) == 0, lows[:, :8], lows[:, 8:]).reshape(256, 128)
    turned = pltpu.roll(both, 64, 1)
    lane = lax.broadcasted_iota(jnp.int32, (128, 256), 0)
    first = jnp.transpose(jnp.where(core == 0, both, turned))
    second = jnp.transpose(jnp.where(core == 0, turned, both))
    spread[:, :256] = jnp.where(lane < 64, first, 0.0).astype(jnp.bfloat16)
    spread[:, 256:] = jnp.where(lane >= 64, second, 0.0).astype(jnp.bfloat16)

    def project(half, z, places=(0, 8)):
        at = half * 2 + z
        begin, end = places
        for k, s in enumerate(chunk(half, z)):
            if not begin <= k < end:
                continue
            update = jnp.dot(slots[s], spread[...], preferred_element_type=jnp.float32)
            for part in range(2):
                rows = pl.ds(pl.multiple_of(s * 160 + part * PACKED, 16), PACKED)
                total = base[rows, :].astype(jnp.float32) + update[:, part * 256:part * 256 + 256]
                merged[at, k * 160 + part * PACKED:k * 160 + part * PACKED + PACKED] = total.astype(jnp.bfloat16)
        columns = slice(begin * 160, end * 160)
        return jnp.dot(ordered[at, :, columns], merged[at, columns], preferred_element_type=jnp.float32)

    query = project(z1, 0) + project(z1, 1)
    pass_straight(down, late_0)
    from_sibling(down, 1)
    query += project(1 - z1, takes)
    pass_rest(down, (2,))
    from_sibling(down, 2)
    query += project(1 - z1, 1 - takes, (0, 4))
    pass_rest(down, (3,))
    from_sibling(down, 3)
    query += project(1 - z1, 1 - takes, (4, 8))

    gains = gain[...]
    heads = []
    for h in range(2):
        head = query[:, h * 128:h * 128 + 128]
        inverse = lax.rsqrt(jnp.mean(head * head, axis=-1, keepdims=True) + 1e-06)
        heads.append(head * inverse * gains)
    tiles = range(4)
    normed = [
        jnp.concatenate([head[j * 8:j * 8 + 8] for head in heads], axis=0).astype(jnp.bfloat16) for j in tiles
    ]
    products = [jnp.dot(normed[j], turned_keys[j], preferred_element_type=jnp.float32) for j in tiles]
    scores = [products[j] * (1.0 / math.sqrt(128)) + bias[j] for j in tiles]
    highest = [jnp.max(scores[j], axis=-1, keepdims=True) for j in tiles]
    expo = [jnp.exp(scores[j] - highest[j]) for j in tiles]
    sums = [jnp.sum(expo[j], axis=-1, keepdims=True) for j in tiles]
    weights = [(expo[j] * (1.0 / sums[j])).astype(jnp.bfloat16) for j in tiles]
    parts = [
        jnp.dot(weights[j], values[j * 8:j * 8 + 8].reshape(512, 128), preferred_element_type=jnp.float32)
        for j in tiles
    ]
    out_ref[...] = jnp.concatenate(
        [jnp.concatenate([part[h * 8:h * 8 + 8] for part in parts], axis=0) for h in range(2)], axis=1
    ).astype(jnp.bfloat16)

    def sent(n, sem):
        for kind in (up, down):
            many(kind, n, sem, recv_core.at[0]).wait_send()

    @pl.when(core == 0)
    def _():
        sent(15, send_dp)

    @pl.when(early_0)
    def _():
        sent(15, send_core)

    @pl.when(late_0)
    def _():
        sent(31, send_core)

    @pl.when(early_1)
    def _():
        sent(16, send_dp)
        sent(16, send_core)
        sent(8, send_pair)

    @pl.when(jnp.logical_and(late, crosses))
    def _():
        sent(16, send_dp)


def local(
    hidden, query_base_matrix, input_side_factor, output_side_factor,
    query_norm_gain, cached_key_heads, cached_value_heads, lengths,
):
    bf16 = jnp.bfloat16
    return pl.pallas_call(
        kernel,
        out_shape=jax.ShapeDtypeStruct((32, 256), bf16),
        in_specs=[pl.BlockSpec(memory_space=pltpu.HBM)] * 8,
        out_specs=pl.BlockSpec(memory_space=pltpu.VMEM),
        scratch_shapes=[
            pltpu.VMEM((32, 5120), bf16),
            pltpu.VMEM((5120, 256), bf16),
            pltpu.VMEM((64, 160), bf16),
            pltpu.VMEM((16, 8, 64), bf16),
            pltpu.VMEM((1, 128), jnp.float32),
            pltpu.VMEM((32, 64, 128), bf16),
            pltpu.VMEM((32, 64, 128), bf16),
            pltpu.VMEM((1, 32), jnp.int32),
            pltpu.VMEM((N_DP, PACKED, 128), bf16),
            pltpu.VMEM((N_DP, GROUP, 128), bf16),
            pltpu.VMEM((2, GROUP, 128), bf16),
            pltpu.VMEM((128, 512), bf16),
            pltpu.VMEM((4, 1280, 256), bf16),
            pltpu.VMEM((4, 32, 1280), bf16),
            pltpu.VMEM((4, 128, 512), bf16),
            pltpu.VMEM((4, 16, 512), jnp.float32),
            pltpu.SemaphoreType.DMA((8,)),
            pltpu.SemaphoreType.DMA((2,)),
            pltpu.SemaphoreType.DMA((2,)),
            pltpu.SemaphoreType.DMA((2,)),
            pltpu.SemaphoreType.DMA((N_DP, 2)),
            pltpu.SemaphoreType.DMA((4, 2)),
        ],
        compiler_params=pltpu.CompilerParams(
            collective_id=0, has_side_effects=True, vmem_limit_bytes=54 * 2**20 - 100_000
        ),
        cost_estimate=pl.CostEstimate(flops=260_000_000, bytes_accessed=4_200_000, transcendentals=32768),
    )(
        hidden, query_base_matrix, input_side_factor.T, jnp.transpose(output_side_factor, (1, 2, 0)),
        query_norm_gain.reshape(1, 128), cached_key_heads.reshape(32, 64, 128),
        cached_value_heads.reshape(32, 64, 128), lengths.reshape(1, 32),
    )


def solution(mesh):
    in_specs = (
        P("dp", None),
        P(None, "tensor"),
        P("dp", None),
        P(None, None, "dp"),
        P(),
        P("dp", "tensor", None, None),
        P("dp", "tensor", None, None),
        P("dp"),
    )
    return jax.shard_map(local, mesh=mesh, in_specs=in_specs, out_specs=P("dp", "tensor"), check_vma=False)
```
